32 devices in a mesh: section: 2 (over y), dp: 8 (over z, x), tensor: 2 (over core).
Axes of the slice: x: 2, y: 2, z: 4, core: 2. Of those that a mesh axis runs over, the one named last changes fastest.
Arguments:
- fwd_input: bfloat16 [2, 256, 2048], P('section', 'dp'), may hold values from -40 to 40
- fresh_input: bfloat16 [256, 2048], P('dp'), may hold values from -40 to 40
- cotangent: bfloat16 [2, 256, 2048], P('section', 'dp'), may hold values from -40 to 40
- fresh_cotangent: bfloat16 [256, 2048], P('dp'), may hold values from -40 to 40
- stash: bfloat16 [2, 2, 256, 2048], P('section', None, 'dp'), may hold values from -40 to 40
- norm_gain: float32 [2, 2048], P('section'), may hold values from 0.25 to 1.75
- qk_gain: float32 [2, 2, 128], P('section'), may hold values from 0.25 to 1.75
- w_query: bfloat16 [2, 2048, 2048], P('section', 'dp', 'tensor'), may hold values from -0.125 to 0.125
- w_key: bfloat16 [2, 2048, 256], P('section', 'dp', 'tensor'), may hold values from -0.125 to 0.125
- w_value: bfloat16 [2, 2048, 256], P('section', 'dp', 'tensor'), may hold values from -0.125 to 0.125
- w_out: bfloat16 [2, 2048, 2048], P('section', 'dp', 'tensor'), may hold values from -0.125 to 0.125
Outputs:
- out_activations: bfloat16 [2, 2, 256, 2048], P('section', None, 'dp')
- grad_input: bfloat16 [2, 2, 256, 2048], P('section', None, 'dp')
- grad_query: float32 [2, 2048, 2048], P('section', 'dp', 'tensor')
- grad_key: float32 [2, 2048, 256], P('section', 'dp', 'tensor')
- grad_value: float32 [2, 2048, 256], P('section', 'dp', 'tensor')
- grad_out: float32 [2, 2048, 2048], P('section', 'dp', 'tensor')
- grad_norm_gain: float32 [2, 2048], P('section')
- grad_qk_gain: float32 [2, 2, 128], P('section')
The draws below stay inside these ranges and needn't reach their ends.
All inputs are finite; a program needn't handle non-finite values.
Results may differ from the reference program's by a relative error of at most 0.02.
Values may be sent and summed in bfloat16 or wider, within the bound.
A program may use at most 64 MiB of HBM per device.

```python
import math
import jax
import jax.numpy as jnp
from jax import lax

D = 2048
HD = 128
HEADS = 16
KV_HEADS = 2
MB = 32
LAYERS = 2
ROWS = 256
WINDOW = 512
N_DP = 8


def activation_draw(key, shape):
    base = jax.random.truncated_normal(jax.random.fold_in(key, 11), -4.0, 4.0, shape, jnp.float32)
    mixed = base
    return jnp.clip(mixed, -40.0, 40.0).astype(jnp.bfloat16)


def draw_fwd_input(key, part):
    return activation_draw(jax.random.fold_in(key, 101), (LAYERS, ROWS, D))


def draw_fresh_input(key, part):
    return activation_draw(jax.random.fold_in(key, 202), (ROWS, D))


def draw_cotangent(key, part):
    return activation_draw(jax.random.fold_in(key, 303), (LAYERS, ROWS, D))


def draw_fresh_cotangent(key, part):
    return activation_draw(jax.random.fold_in(key, 404), (ROWS, D))


def draw_stash(key, part):
    return activation_draw(jax.random.fold_in(key, 505), (LAYERS, 2, ROWS, D))


def level_of(key, dims, shards, low, largest):
    gain = 1.0
    for position, blocks in shards:
        draws = jax.random.uniform(jax.random.fold_in(jax.random.fold_in(key, 6), position), (blocks,), jnp.float32, low / len(shards), largest / len(shards))
        gain = gain * jnp.repeat(jnp.exp(draws), dims[position] // blocks).reshape((-1,) + (1,) * (len(dims) - 1 - position))
    return gain


def scatter_about(key, extent, deviation, reach, cuts=(), held_as=jnp.bfloat16):
    drawn = deviation * jax.random.normal(key, extent, jnp.float32)
    if cuts:
        drawn = drawn * level_of(key, extent, cuts, -0.22, 0.18)
    return jnp.clip(drawn, -reach, reach).astype(held_as)


def setup_inputs(seed: int = 0) -> dict:
    key_list = jax.random.split(jax.random.key(seed), 12)
    return {
        "fwd_input": draw_fwd_input(jax.random.fold_in(key_list[11], 71), 0),
        "fresh_input": draw_fresh_input(jax.random.fold_in(key_list[11], 71), 0),
        "cotangent": draw_cotangent(jax.random.fold_in(key_list[11], 71), 0),
        "fresh_cotangent": draw_fresh_cotangent(jax.random.fold_in(key_list[11], 71), 0),
        "stash": draw_stash(jax.random.fold_in(key_list[11], 71), 0),
        "norm_gain": jnp.clip(1.0 + 0.15 * jax.random.normal(key_list[5], (LAYERS, D), jnp.float32), 0.25, 1.75),
        "qk_gain": jnp.clip(1.0 + 0.15 * jax.random.normal(key_list[6], (LAYERS, 2, HD), jnp.float32), 0.25, 1.75),
        "w_query": scatter_about(key_list[7], (LAYERS, D, HEADS * HD), D ** -0.5, 0.125, ((0, 2), (1, 8), (2, 2))),
        "w_key": scatter_about(key_list[8], (LAYERS, D, KV_HEADS * HD), D ** -0.5, 0.125, ((0, 2), (1, 8), (2, 2))),
        "w_value": scatter_about(key_list[9], (LAYERS, D, KV_HEADS * HD), D ** -0.5, 0.125, ((0, 2), (1, 8), (2, 2))),
        "w_out": scatter_about(key_list[10], (LAYERS, D, HEADS * HD), (HEADS * HD) ** -0.5, 0.125, ((0, 2), (1, 8), (2, 2))),
    }


EPSILON = 1e-06
THETA = 1000000.0

def rope_tables(length, width):
    half_width = width // 2
    freqs = jnp.exp(jnp.arange(half_width, dtype=jnp.float32) * (-2.0 * math.log(THETA) / width))
    angles = jnp.arange(length, dtype=jnp.float32)[:, None] * freqs[None, :]
    return (jnp.cos(angles), jnp.sin(angles))

def rotate(vectors, cos_tab, sin_tab):
    half_width = vectors.shape[-1] // 2
    first_half = vectors[..., :half_width]
    second_half = vectors[..., half_width:]
    cos_here = cos_tab[:, None, :]
    sin_here = sin_tab[:, None, :]
    return jnp.concatenate([first_half * cos_here - second_half * sin_here, second_half * cos_here + first_half * sin_here], axis=-1)

def head_norm(raw_heads):
    inverse = lax.rsqrt(lax.optimization_barrier(jnp.mean(raw_heads * raw_heads, axis=-1, keepdims=True)) + EPSILON)
    return (raw_heads * inverse, inverse)

def unit_back(grad_unit, unit_row_vectors, inverse):
    return inverse * (grad_unit - unit_row_vectors * lax.optimization_barrier(jnp.mean(grad_unit * unit_row_vectors, axis=-1, keepdims=True)))

def attend_full(normed, w_q, w_k, w_v, qk_gains, cos_tab, sin_tab):
    row_count = normed.shape[0]
    group_size = HEADS // KV_HEADS
    q_unit, q_inv = head_norm(jnp.dot(normed, w_q, preferred_element_type=jnp.float32).reshape(row_count, HEADS, HD))
    k_unit, k_inv = head_norm(jnp.dot(normed, w_k, preferred_element_type=jnp.float32).reshape(row_count, KV_HEADS, HD))
    queries = rotate(q_unit * qk_gains[0], cos_tab, sin_tab).astype(jnp.bfloat16).reshape(row_count, KV_HEADS, group_size, HD)
    keys_b = rotate(k_unit * qk_gains[1], cos_tab, sin_tab).astype(jnp.bfloat16)
    values_b = jnp.dot(normed, w_v, preferred_element_type=jnp.float32).astype(jnp.bfloat16).reshape(row_count, KV_HEADS, HD)
    scores = jnp.einsum('qkgd,tkd->kgqt', queries.astype(jnp.float32), keys_b.astype(jnp.float32)) * (1.0 / math.sqrt(HD))
    causal = lax.broadcasted_iota(jnp.int32, (row_count, row_count), 0) >= lax.broadcasted_iota(jnp.int32, (row_count, row_count), 1)
    expd = jnp.where(causal, jnp.exp(scores), 0.0)
    softmax_f = expd / lax.optimization_barrier(jnp.sum(expd, axis=-1, keepdims=True))
    softmax_b = softmax_f.astype(jnp.bfloat16)
    attended = jnp.einsum('kgqt,tkd->qkgd', softmax_b.astype(jnp.float32), values_b.astype(jnp.float32))
    attended = attended.reshape(row_count, HEADS * HD).astype(jnp.bfloat16)
    return (q_unit, q_inv, k_unit, k_inv, queries, keys_b, values_b, softmax_f, softmax_b, attended)

def input_norm(x_rows, norm_scale):
    x_float = x_rows.astype(jnp.float32)
    inverse = lax.rsqrt(lax.optimization_barrier(jnp.mean(x_float * x_float, axis=-1, keepdims=True)) + EPSILON)
    unit_row_vectors = x_float * inverse
    return (x_float, inverse, unit_row_vectors, (unit_row_vectors * norm_scale).astype(jnp.bfloat16))

def layer_forward(x_rows, norm_scale, w_q, w_k, w_v, w_o, qk_gains, cos_tab, sin_tab):
    x_float, inverse, unit_row_vectors, normed = input_norm(x_rows, norm_scale)
    attended = attend_full(normed, w_q, w_k, w_v, qk_gains, cos_tab, sin_tab)[-1]
    mixed = lax.dot_general(attended, w_o, (((1,), (1,)), ((), ())), preferred_element_type=jnp.float32)
    return (x_float + mixed).astype(jnp.bfloat16)

def layer_backward(x_rows, cot_rows, norm_scale, w_q, w_k, w_v, w_o, qk_gains, cos_tab, sin_tab):
    x_float, inverse, unit_row_vectors, normed = input_norm(x_rows, norm_scale)
    q_unit, q_inv, k_unit, k_inv, queries, keys_b, values_b, softmax_f, softmax_b, attended = attend_full(normed, w_q, w_k, w_v, qk_gains, cos_tab, sin_tab)
    row_count = x_rows.shape[0]
    group_size = HEADS // KV_HEADS
    d_attn = jnp.dot(cot_rows, w_o, preferred_element_type=jnp.float32).astype(jnp.bfloat16).reshape(row_count, KV_HEADS, group_size, HD)
    d_probs = jnp.einsum('qkgd,tkd->kgqt', d_attn.astype(jnp.float32), values_b.astype(jnp.float32))
    d_value = jnp.einsum('kgqt,qkgd->tkd', softmax_b.astype(jnp.float32), d_attn.astype(jnp.float32))
    d_value = d_value.astype(jnp.bfloat16).reshape(row_count, KV_HEADS * HD)
    d_scores = softmax_f * (d_probs - lax.optimization_barrier(jnp.sum(softmax_f * d_probs, axis=-1, keepdims=True))) * (1.0 / math.sqrt(HD))
    d_scores = d_scores.astype(jnp.bfloat16).astype(jnp.float32)
    d_query = jnp.einsum('kgqt,tkd->qkgd', d_scores, keys_b.astype(jnp.float32)).reshape(row_count, HEADS, HD)
    d_key = jnp.einsum('kgqt,qkgd->tkd', d_scores, queries.astype(jnp.float32))
    d_query = rotate(d_query, cos_tab, -sin_tab)
    d_key = rotate(d_key, cos_tab, -sin_tab)
    q_term = lax.optimization_barrier(jnp.sum(d_query * q_unit, axis=(0, 1)))
    k_term = lax.optimization_barrier(jnp.sum(d_key * k_unit, axis=(0, 1)))
    q_grad = unit_back(d_query * qk_gains[0], q_unit, q_inv).astype(jnp.bfloat16).reshape(row_count, HEADS * HD)
    k_grad = unit_back(d_key * qk_gains[1], k_unit, k_inv).astype(jnp.bfloat16).reshape(row_count, KV_HEADS * HD)
    contract = (((1,), (1,)), ((), ()))
    d_normed = lax.dot_general(q_grad, w_q, contract, preferred_element_type=jnp.float32)
    d_normed = d_normed + lax.dot_general(k_grad, w_k, contract, preferred_element_type=jnp.float32)
    d_normed = d_normed + lax.dot_general(d_value, w_v, contract, preferred_element_type=jnp.float32)
    norm_term = lax.optimization_barrier(jnp.sum(d_normed * unit_row_vectors, axis=0))
    d_input = (cot_rows.astype(jnp.float32) + unit_back(d_normed * norm_scale, unit_row_vectors, inverse)).astype(jnp.bfloat16)
    columns = jnp.concatenate([q_grad, k_grad, d_value], axis=1)
    return (d_input, normed, columns, attended, norm_term, q_term, k_term)

def reference(fwd_input, fresh_input, cotangent, fresh_cotangent, stash, norm_gain, qk_gain, w_query, w_key, w_value, w_out):
    cos_tab, sin_tab = rope_tables(MB, HD)
    grad_scale = 1.0 / math.sqrt(WINDOW)

    def as_blocks(array):
        return array.reshape(N_DP, MB, D)

    def forward_section(section_id, blocks_in):

        def apply_one(rows_in):
            return layer_forward(rows_in, norm_gain[section_id], w_query[section_id], w_key[section_id], w_value[section_id], w_out[section_id], qk_gain[section_id], cos_tab, sin_tab)
        return jax.vmap(apply_one)(blocks_in)

    def backward_section(section_id, blocks_in, blocks_cot):

        def apply_one(rows_in, rows_cot):
            return layer_backward(rows_in, rows_cot, norm_gain[section_id], w_query[section_id], w_key[section_id], w_value[section_id], w_out[section_id], qk_gain[section_id], cos_tab, sin_tab)
        return jax.vmap(apply_one)(blocks_in, blocks_cot)
    first_out = [forward_section(section_id, as_blocks(fwd_input[section_id])) for section_id in range(LAYERS)]
    second_in = [as_blocks(fresh_input)] + first_out[:-1]
    second_out = [forward_section(section_id, second_in[section_id]) for section_id in range(LAYERS)]
    mirrored = stash[::-1]
    first_back = [backward_section(section_id, as_blocks(mirrored[section_id, 0]), as_blocks(cotangent[section_id])) for section_id in range(LAYERS)]
    second_cot = [first_back[section_id + 1][0] for section_id in range(LAYERS - 1)] + [as_blocks(fresh_cotangent)]
    second_back = [backward_section(section_id, as_blocks(mirrored[section_id, 1]), second_cot[section_id]) for section_id in range(LAYERS)]
    width_all = 2 * HEADS * HD + 2 * KV_HEADS * HD
    q_width = HEADS * HD
    k_width = KV_HEADS * HD

    def add_block(running, block_items):
        normed_b, cols_b, cots_b, att_b = block_items
        contract = (((0,), (0,)), ((), ()))
        left_term = lax.dot_general(normed_b, cols_b, contract, preferred_element_type=jnp.float32)
        right_term = lax.dot_general(cots_b, att_b, contract, preferred_element_type=jnp.float32)
        partial_b = (jnp.concatenate([left_term, right_term], axis=1) * grad_scale).astype(jnp.bfloat16)
        partial_b = lax.optimization_barrier(partial_b)
        return (running + partial_b.astype(jnp.float32), None)
    grads_q, key_gradients, value_gradients, grads_o, grads_norm, grads_qk = ([], [], [], [], [], [])
    for section_id in range(LAYERS):
        fb = first_back[section_id]
        sb = second_back[section_id]
        normed_rows = jnp.concatenate([fb[1], sb[1]], axis=1)
        col_rows = jnp.concatenate([fb[2], sb[2]], axis=1)
        cot_rows = jnp.concatenate([as_blocks(cotangent[section_id]), second_cot[section_id]], axis=1)
        att_rows = jnp.concatenate([fb[3], sb[3]], axis=1)
        summed, unused = lax.scan(add_block, jnp.zeros((D, width_all), jnp.float32), (normed_rows, col_rows, cot_rows, att_rows))
        grads_q.append(summed[:, :q_width])
        key_gradients.append(summed[:, q_width:q_width + k_width])
        value_gradients.append(summed[:, q_width + k_width:q_width + 2 * k_width])
        grads_o.append(summed[:, q_width + 2 * k_width:])
        grads_norm.append(grad_scale * lax.optimization_barrier(jnp.sum(fb[4] + sb[4], axis=0)))
        grads_qk.append(grad_scale * jnp.stack([lax.optimization_barrier(jnp.sum(fb[5] + sb[5], axis=0)), lax.optimization_barrier(jnp.sum(fb[6] + sb[6], axis=0))]))
    out_activations = jnp.stack([jnp.stack([first_out[section_id], second_out[section_id]]) for section_id in range(LAYERS)]).reshape(LAYERS, 2, ROWS, D)
    grad_input = jnp.stack([jnp.stack([first_back[section_id][0], second_back[section_id][0]]) for section_id in range(LAYERS)]).reshape(LAYERS, 2, ROWS, D)
    return (out_activations, grad_input, jnp.stack(grads_q), jnp.stack(key_gradients), jnp.stack(value_gradients), jnp.stack(grads_o), jnp.stack(grads_norm), jnp.stack(grads_qk))
```

```python
import math

import jax
import jax.numpy as jnp
from jax import lax
from jax.sharding import PartitionSpec as P

HD = 128


EPSILON = 1e-06
THETA = 1000000.0


def swapped(block, axis, apart):
    count = lax.axis_size(axis)
    route = []
    for low in range(count):
        high = low | 1 << apart
        if high != low and high < count:
            route += [(low, high), (high, low)]
    return lax.ppermute(block, axis, route)


def passed_along(array, axis, by):
    count = lax.axis_size(axis)
    pairs = [(i, i + by) for i in range(count) if 0 <= i + by < count]
    return lax.ppermute(array, axis, pairs)


def rope_tables(length, width):
    half_width = width // 2
    freqs = jnp.exp(jnp.arange(half_width, dtype=jnp.float32) * (-2.0 * math.log(THETA) / width))
    angles = jnp.arange(length, dtype=jnp.float32)[:, None] * freqs[None, :]
    return (jnp.cos(angles), jnp.sin(angles))


def rotate(vectors, cos_tab, sin_tab):
    half_width = vectors.shape[-1] // 2
    first_half = vectors[..., :half_width]
    second_half = vectors[..., half_width:]
    cos_here = cos_tab[:, None, :]
    sin_here = sin_tab[:, None, :]
    return jnp.concatenate(
        [
            first_half * cos_here - second_half * sin_here,
            second_half * cos_here + first_half * sin_here,
        ],
        axis=-1,
    )


def head_norm(raw_heads):
    inverse = lax.rsqrt(jnp.mean(raw_heads * raw_heads, axis=-1, keepdims=True) + EPSILON)
    return (raw_heads * inverse, inverse)


def unit_back(grad_unit, unit_row_vectors, inverse):
    return inverse * (
        grad_unit
        - unit_row_vectors * jnp.mean(grad_unit * unit_row_vectors, axis=-1, keepdims=True)
    )


def input_norm(x_rows, norm_scale):
    x_float = x_rows.astype(jnp.float32)
    inverse = lax.rsqrt(jnp.mean(x_float * x_float, axis=-1, keepdims=True) + EPSILON)
    unit_row_vectors = x_float * inverse
    return (
        x_float,
        inverse,
        unit_row_vectors,
        (unit_row_vectors * norm_scale).astype(jnp.bfloat16),
    )


def attend_local(normed, w_q, w_k, w_v, qk_gains, cos_tab, sin_tab):
    row_count = normed.shape[0]
    head_count = w_q.shape[1] // HD
    kv_count = w_k.shape[1] // HD
    group_size = head_count // kv_count
    q_unit, q_inv = head_norm(
        jnp.dot(normed, w_q, preferred_element_type=jnp.float32).reshape(row_count, head_count, HD)
    )
    k_unit, k_inv = head_norm(
        jnp.dot(normed, w_k, preferred_element_type=jnp.float32).reshape(row_count, kv_count, HD)
    )
    queries = (
        rotate(q_unit * qk_gains[0], cos_tab, sin_tab)
        .astype(jnp.bfloat16)
        .reshape(row_count, kv_count, group_size, HD)
    )
    keys_b = rotate(k_unit * qk_gains[1], cos_tab, sin_tab).astype(jnp.bfloat16)
    values_b = (
        jnp.dot(normed, w_v, preferred_element_type=jnp.float32)
        .astype(jnp.bfloat16)
        .reshape(row_count, kv_count, HD)
    )
    scores = jnp.einsum("qkgd,tkd->kgqt", queries, keys_b, preferred_element_type=jnp.float32) * (
        1.0 / math.sqrt(HD)
    )
    causal = lax.broadcasted_iota(jnp.int32, (row_count, row_count), 0) >= lax.broadcasted_iota(
        jnp.int32, (row_count, row_count), 1
    )
    expd = jnp.where(causal, jnp.exp(scores), 0.0)
    softmax_f = expd / jnp.sum(expd, axis=-1, keepdims=True)
    softmax_b = softmax_f.astype(jnp.bfloat16)
    attended = jnp.einsum("kgqt,tkd->qkgd", softmax_b, values_b, preferred_element_type=jnp.float32)
    attended = attended.reshape(row_count, head_count * HD).astype(jnp.bfloat16)
    return (q_unit, q_inv, k_unit, k_inv, queries, keys_b, values_b, softmax_f, softmax_b, attended)


def forward_part(x_rows, norm_scale, weights, qk_gains, cos_tab, sin_tab):
    w_q, w_k, w_v, w_o = weights
    x_float, inverse, unit_row_vectors, normed = input_norm(x_rows, norm_scale)
    attended = attend_local(normed, w_q, w_k, w_v, qk_gains, cos_tab, sin_tab)[-1]
    out_part = lax.dot_general(
        attended, w_o, (((1,), (1,)), ((), ())), preferred_element_type=jnp.float32
    )
    return (x_float, out_part)


def backward_part(x_rows, cot_rows, norm_scale, weights, qk_gains, cos_tab, sin_tab):
    w_q, w_k, w_v, w_o = weights
    x_float, inverse, unit_row_vectors, normed = input_norm(x_rows, norm_scale)
    q_unit, q_inv, k_unit, k_inv, queries, keys_b, values_b, softmax_f, softmax_b, attended = (
        attend_local(normed, w_q, w_k, w_v, qk_gains, cos_tab, sin_tab)
    )
    row_count, kv_count, group_size = (queries.shape[0], queries.shape[1], queries.shape[2])
    d_attn = (
        jnp.dot(cot_rows, w_o, preferred_element_type=jnp.float32)
        .astype(jnp.bfloat16)
        .reshape(row_count, kv_count, group_size, HD)
    )
    d_probs = jnp.einsum("qkgd,tkd->kgqt", d_attn, values_b, preferred_element_type=jnp.float32)
    d_value = jnp.einsum("kgqt,qkgd->tkd", softmax_b, d_attn, preferred_element_type=jnp.float32)
    d_value = d_value.astype(jnp.bfloat16).reshape(row_count, kv_count * HD)
    d_scores = (
        softmax_f
        * (d_probs - jnp.sum(softmax_f * d_probs, axis=-1, keepdims=True))
        * (1.0 / math.sqrt(HD))
    )
    d_scores = d_scores.astype(jnp.bfloat16)
    d_query = jnp.einsum(
        "kgqt,tkd->qkgd", d_scores, keys_b, preferred_element_type=jnp.float32
    ).reshape(row_count, kv_count * group_size, HD)
    d_key = jnp.einsum("kgqt,qkgd->tkd", d_scores, queries, preferred_element_type=jnp.float32)
    d_query = rotate(d_query, cos_tab, -sin_tab)
    d_key = rotate(d_key, cos_tab, -sin_tab)
    q_term = jnp.sum(d_query * q_unit, axis=(0, 1))
    k_term = jnp.sum(d_key * k_unit, axis=(0, 1))
    q_grad = (
        unit_back(d_query * qk_gains[0], q_unit, q_inv).astype(jnp.bfloat16).reshape(row_count, -1)
    )
    k_grad = (
        unit_back(d_key * qk_gains[1], k_unit, k_inv).astype(jnp.bfloat16).reshape(row_count, -1)
    )
    contract = (((1,), (1,)), ((), ()))
    normed_part = lax.dot_general(q_grad, w_q, contract, preferred_element_type=jnp.float32)
    normed_part = normed_part + lax.dot_general(
        k_grad, w_k, contract, preferred_element_type=jnp.float32
    )
    normed_part = normed_part + lax.dot_general(
        d_value, w_v, contract, preferred_element_type=jnp.float32
    )
    columns = jnp.concatenate([q_grad, k_grad, d_value], axis=1)
    return (normed_part, unit_row_vectors, inverse, normed, columns, attended, q_term, k_term)


def tensor_sum(part):
    count = lax.axis_size("tensor")
    mine = part.astype(jnp.bfloat16)
    total = mine.astype(jnp.float32)
    for step in range(1, count):
        route = [(i, i ^ step) for i in range(count)]
        total = total + lax.ppermute(mine, "tensor", route).astype(jnp.float32)
    return total


def tensor_sums(out_part, normed_part):
    both = tensor_sum(jnp.concatenate([out_part, normed_part], axis=0))
    rows = out_part.shape[0]
    return both[:rows], both[rows:]


def run_slot(x_forward, x_backward, cot_rows, norm_scale, weights, qk_gains, cos_tab, sin_tab):
    x_float, out_part = forward_part(x_forward, norm_scale, weights, qk_gains, cos_tab, sin_tab)
    normed_part, unit_row_vectors, inverse, normed, columns, attended, q_term, k_term = (
        backward_part(x_backward, cot_rows, norm_scale, weights, qk_gains, cos_tab, sin_tab)
    )
    out_sum, d_normed = tensor_sums(out_part, normed_part)
    layer_out = (x_float + out_sum).astype(jnp.bfloat16)
    d_input = (
        cot_rows.astype(jnp.float32) + unit_back(d_normed * norm_scale, unit_row_vectors, inverse)
    ).astype(jnp.bfloat16)
    norm_term = jnp.sum(d_normed * unit_row_vectors, axis=0)
    return (layer_out, d_input, normed, columns, attended, norm_term, q_term, k_term)


def local(
    fwd_input,
    fresh_input,
    cotangent,
    fresh_cotangent,
    stash,
    norm_gain,
    qk_gain,
    w_query,
    w_key,
    w_value,
    w_out,
):
    full_q, full_k, full_v, full_o = (
        lax.all_gather(w_query, "dp", axis=1, tiled=True),
        lax.all_gather(w_key, "dp", axis=1, tiled=True),
        lax.all_gather(w_value, "dp", axis=1, tiled=True),
        lax.all_gather(w_out, "dp", axis=1, tiled=True),
    )
    weights = (full_q[0], full_k[0], full_v[0], full_o[0])
    norm_scale = norm_gain[0]
    qk_gains = qk_gain[0]
    row_count = fwd_input.shape[1]
    cos_tab, sin_tab = rope_tables(row_count, HD)
    section_position_index = lax.axis_index("section")
    section_total = lax.axis_size("section")
    bit_order = list(range(section_total.bit_length() - 1))
    reloaded = stash[0]
    for bit_index in bit_order:
        reloaded = swapped(reloaded, "section", bit_index)
    first_slot = run_slot(
        fwd_input[0], reloaded[0], cotangent[0], norm_scale, weights, qk_gains, cos_tab, sin_tab
    )
    arrived = passed_along(first_slot[0], "section", 1)
    second_input = jnp.where(section_position_index == 0, fresh_input, arrived)
    returned = passed_along(first_slot[1], "section", -1)
    second_cot = jnp.where(section_position_index == section_total - 1, fresh_cotangent, returned)
    second_slot = run_slot(
        second_input, reloaded[1], second_cot, norm_scale, weights, qk_gains, cos_tab, sin_tab
    )
    out_activations = jnp.stack([first_slot[0], second_slot[0]])[None]
    grad_input = jnp.stack([first_slot[1], second_slot[1]])[None]
    grad_scale = 1.0 / math.sqrt(2 * row_count * lax.axis_size("dp"))
    normed_rows = jnp.concatenate([first_slot[2], second_slot[2]], axis=0)
    column_rows = jnp.concatenate([first_slot[3], second_slot[3]], axis=0)
    cot_rows = jnp.concatenate([cotangent[0], second_cot], axis=0)
    attended_rows = jnp.concatenate([first_slot[4], second_slot[4]], axis=0)
    contract = (((0,), (0,)), ((), ()))
    sliced = lax.all_to_all(
        jnp.stack([normed_rows, cot_rows]), "dp", split_axis=2, concat_axis=1, tiled=True
    )
    gathered = lax.all_gather(
        jnp.concatenate([column_rows, attended_rows], axis=1), "dp", axis=0, tiled=True
    )
    left_width = column_rows.shape[1]
    left_term = lax.dot_general(
        sliced[0], gathered[:, :left_width], contract, preferred_element_type=jnp.float32
    )
    right_term = lax.dot_general(
        sliced[1], gathered[:, left_width:], contract, preferred_element_type=jnp.float32
    )
    left_term = left_term * grad_scale
    right_term = right_term * grad_scale
    q_width = w_query.shape[2]
    k_width = w_key.shape[2]
    grad_query = left_term[:, :q_width][None]
    grad_key = left_term[:, q_width : q_width + k_width][None]
    grad_value = left_term[:, q_width + k_width :][None]
    grad_out = right_term[None]
    norm_term = first_slot[5] + second_slot[5]
    feature_count = norm_term.shape[0]
    half_width = feature_count // lax.axis_size("tensor")
    feature_owner = lax.broadcasted_iota(jnp.int32, (feature_count,), 0) // half_width
    own_half = jnp.where(feature_owner == lax.axis_index("tensor"), norm_term, 0.0)
    qk_term = jnp.stack([first_slot[6] + second_slot[6], first_slot[7] + second_slot[7]])
    norm_total, qk_total = lax.psum((own_half * grad_scale, qk_term * grad_scale), ("dp", "tensor"))
    return (
        out_activations,
        grad_input,
        grad_query,
        grad_key,
        grad_value,
        grad_out,
        norm_total[None],
        qk_total[None],
    )


def solution(mesh):
    return jax.shard_map(
        local,
        mesh=mesh,
        in_specs=(
            P("section", "dp", None),
            P("dp", None),
            P("section", "dp", None),
            P("dp", None),
            P("section", None, "dp", None),
            P("section", None),
            P("section", None, None),
            P("section", "dp", "tensor"),
            P("section", "dp", "tensor"),
            P("section", "dp", "tensor"),
            P("section", "dp", "tensor"),
        ),
        out_specs=(
            P("section", None, "dp", None),
            P("section", None, "dp", None),
            P("section", "dp", "tensor"),
            P("section", "dp", "tensor"),
            P("section", "dp", "tensor"),
            P("section", "dp", "tensor"),
            P("section", None),
            P("section", None, None),
        ),
        check_vma=False,
    )
```

```python
import functools
import math

import jax
import jax.numpy as jnp
from jax import lax
from jax.experimental import pallas as pl
from jax.experimental.pallas import tpu as pltpu
from jax.sharding import PartitionSpec as P

HD = 128


EPSILON = 1e-06
THETA = 1000000.0


def swapped(block, axis, apart):
    count = lax.axis_size(axis)
    route = []
    for low in range(count):
        high = low | 1 << apart
        if high != low and high < count:
            route += [(low, high), (high, low)]
    return lax.ppermute(block, axis, route)


def passed_along(array, axis, by):
    count = lax.axis_size(axis)
    pairs = [(i, i + by) for i in range(count) if 0 <= i + by < count]
    return lax.ppermute(array, axis, pairs)


def grid_of(count):
    tall = 4 if count % 4 == 0 else 1
    return tall, count // tall


def meet(peers):
    barrier = pltpu.get_barrier_semaphore()
    for peer in peers:
        pl.semaphore_signal(barrier, inc=1, device_id=peer)
    pl.semaphore_wait(barrier, len(peers))


class Sends:
    def __init__(self, sems):
        self.sems = sems
        self.started = []

    def start(self, src, dst, recv, peer):
        copy = pltpu.make_async_remote_copy(
            src_ref=src,
            dst_ref=dst,
            send_sem=self.sems.at[len(self.started)],
            recv_sem=recv,
            device_id=peer,
        )
        copy.start()
        self.started.append(copy)

    def arrived(self, dst, recv, peer):
        pltpu.make_async_remote_copy(
            src_ref=dst, dst_ref=dst, send_sem=self.sems.at[0], recv_sem=recv, device_id=peer
        ).wait_recv()

    def finish(self):
        for copy in self.started:
            copy.wait_send()


def neighbours(count):
    tall, wide = grid_of(count)
    me = lax.axis_index("dp")
    row, col = me // wide, me % wide
    across = [row * wide + (col + i) % wide for i in range(1, wide)]
    along = [((row + i) % tall) * wide + col for i in range(1, tall)]
    return me, row, across, along


def spread(sends, pieces, me, across, along, recv):
    for c, (src, dst) in enumerate(pieces):
        for peer in along + across:
            sends.start(src, dst(me), recv.at[me, c], {"dp": peer})


def relay(sends, pieces, c, across, along, recv):
    dst = pieces[c][1]
    for peer in along:
        sends.arrived(dst(peer), recv.at[peer, c], {"dp": peer})
        for other in across:
            sends.start(dst(peer), dst(peer), recv.at[peer, c], {"dp": other})


def collect(sends, pieces, c, row, count, across, recv):
    tall, wide = grid_of(count)
    dst = pieces[c][1]
    for other in across:
        for i in range(tall):
            shard = ((row + i) % tall) * wide + other % wide
            sends.arrived(dst(shard), recv.at[shard, c], {"dp": other})


def halves(src, full, depth):
    half = depth // 2
    return [
        (src.at[pl.ds(i * half, half)], lambda j, i=i: full.at[j, pl.ds(i * half, half)])
        for i in range(2)
    ]


def weights_kernel(count, in_ref, out_ref, full_in, full_out, send, recv, own):
    me, row, across, along = neighbours(count)
    depth = in_ref.shape[0]
    meet([{"dp": j} for j in along + across])
    pieces = halves(in_ref, full_in, depth) + halves(out_ref, full_out, depth)
    sends = Sends(send)
    spread(sends, pieces, me, across, along, recv)
    mine = [
        pltpu.make_async_copy(in_ref, full_in.at[me], own.at[0]),
        pltpu.make_async_copy(out_ref, full_out.at[me], own.at[1]),
    ]
    for copy in mine:
        copy.start()
    for c in range(len(pieces)):
        relay(sends, pieces, c, across, along, recv)
    for c in range(len(pieces)):
        collect(sends, pieces, c, row, count, across, recv)
    for copy in mine:
        copy.wait()
    sends.finish()


def grads_kernel(count, cols_ref, acts_ref, small_ref, full, sliced, smalls, send, recv, own):
    me, row, across, along = neighbours(count)
    core = lax.axis_index("tensor")
    depth = sliced.shape[-1]
    everyone = [{"dp": (me + i) % count} for i in range(1, count)]
    crossed = [{"dp": (me + i) % count, "tensor": 1 - core} for i in range(count)]
    meet(everyone + crossed)
    pieces = halves(cols_ref, full, cols_ref.shape[0])
    sends = Sends(send)
    spread(sends, pieces, me, across, along, recv)
    for peer in everyone:
        block = pl.ds(pl.multiple_of(peer["dp"] * depth, depth), depth)
        sends.start(acts_ref.at[:, :, block], sliced.at[me], recv.at[me, 2], peer)
    for peer in everyone + crossed:
        sends.start(small_ref, smalls.at[core, me], recv.at[me, 3 + core], peer)
    block = pl.ds(pl.multiple_of(me * depth, depth), depth)
    mine = [
        pltpu.make_async_copy(cols_ref, full.at[me], own.at[0]),
        pltpu.make_async_copy(acts_ref.at[:, :, block], sliced.at[me], own.at[1]),
        pltpu.make_async_copy(small_ref, smalls.at[core, me], own.at[2]),
    ]
    for copy in mine:
        copy.start()
    for c in range(2):
        relay(sends, pieces, c, across, along, recv)
    for c in range(2):
        collect(sends, pieces, c, row, count, across, recv)
    for peer in everyone:
        j = peer["dp"]
        sends.arrived(sliced.at[j], recv.at[j, 2], peer)
        sends.arrived(smalls.at[core, j], recv.at[j, 3 + core], peer)
    for peer in crossed:
        j = peer["dp"]
        sends.arrived(smalls.at[1 - core, j], recv.at[j, 4 - core], peer)
    for copy in mine:
        copy.wait()
    sends.finish()


ANY = pl.BlockSpec(memory_space=pl.ANY)


def gather_weights(w_in, w_out):
    count = lax.axis_size("dp")
    tall, wide = grid_of(count)
    sent = 4 * (tall + wide - 2 + (tall - 1) * (wide - 1))
    return pl.pallas_call(
        functools.partial(weights_kernel, count),
        out_shape=[jax.ShapeDtypeStruct((count,) + w.shape, w.dtype) for w in (w_in, w_out)],
        in_specs=[ANY] * 2,
        out_specs=[ANY] * 2,
        scratch_shapes=[
            pltpu.SemaphoreType.DMA((sent,)),
            pltpu.SemaphoreType.DMA((count, 4)),
            pltpu.SemaphoreType.DMA((2,)),
        ],
        compiler_params=pltpu.CompilerParams(collective_id=0, has_side_effects=True),
    )(w_in, w_out)


def exchange_grads(cols, acts, small):
    count = lax.axis_size("dp")
    tall, wide = grid_of(count)
    rows, width = acts.shape[1:]
    sent = 2 * (tall + wide - 2 + (tall - 1) * (wide - 1)) + 3 * count - 2
    return pl.pallas_call(
        functools.partial(grads_kernel, count),
        out_shape=[
            jax.ShapeDtypeStruct((count,) + cols.shape, cols.dtype),
            jax.ShapeDtypeStruct((count, 2, rows, width // count), acts.dtype),
            jax.ShapeDtypeStruct((2, count) + small.shape, small.dtype),
        ],
        in_specs=[ANY] * 3,
        out_specs=[ANY] * 3,
        scratch_shapes=[
            pltpu.SemaphoreType.DMA((sent,)),
            pltpu.SemaphoreType.DMA((count, 5)),
            pltpu.SemaphoreType.DMA((3,)),
        ],
        compiler_params=pltpu.CompilerParams(collective_id=1, has_side_effects=True),
    )(cols, acts, small)


def rope_tables(length, width):
    half_width = width // 2
    freqs = jnp.exp(jnp.arange(half_width, dtype=jnp.float32) * (-2.0 * math.log(THETA) / width))
    angles = jnp.arange(length, dtype=jnp.float32)[:, None] * freqs[None, :]
    return (jnp.cos(angles), jnp.sin(angles))


def rotate(vectors, cos_tab, sin_tab):
    half_width = vectors.shape[-1] // 2
    first_half = vectors[..., :half_width]
    second_half = vectors[..., half_width:]
    cos_here = cos_tab[:, None, :]
    sin_here = sin_tab[:, None, :]
    return jnp.concatenate(
        [
            first_half * cos_here - second_half * sin_here,
            second_half * cos_here + first_half * sin_here,
        ],
        axis=-1,
    )


def head_norm(raw_heads):
    inverse = lax.rsqrt(jnp.mean(raw_heads * raw_heads, axis=-1, keepdims=True) + EPSILON)
    return (raw_heads * inverse, inverse)


def unit_back(grad_unit, unit_row_vectors, inverse):
    return inverse * (
        grad_unit
        - unit_row_vectors * jnp.mean(grad_unit * unit_row_vectors, axis=-1, keepdims=True)
    )


def input_norm(x_rows, norm_scale):
    x_float = x_rows.astype(jnp.float32)
    inverse = lax.rsqrt(jnp.mean(x_float * x_float, axis=-1, keepdims=True) + EPSILON)
    unit_row_vectors = x_float * inverse
    return (
        x_float,
        inverse,
        unit_row_vectors,
        (unit_row_vectors * norm_scale).astype(jnp.bfloat16),
    )


def attend_local(normed, w_q, w_k, w_v, qk_gains, cos_tab, sin_tab):
    row_count = normed.shape[0]
    head_count = w_q.shape[1] // HD
    kv_count = w_k.shape[1] // HD
    group_size = head_count // kv_count
    q_unit, q_inv = head_norm(
        jnp.dot(normed, w_q, preferred_element_type=jnp.float32).reshape(row_count, head_count, HD)
    )
    k_unit, k_inv = head_norm(
        jnp.dot(normed, w_k, preferred_element_type=jnp.float32).reshape(row_count, kv_count, HD)
    )
    queries = (
        rotate(q_unit * qk_gains[0], cos_tab, sin_tab)
        .astype(jnp.bfloat16)
        .reshape(row_count, kv_count, group_size, HD)
    )
    keys_b = rotate(k_unit * qk_gains[1], cos_tab, sin_tab).astype(jnp.bfloat16)
    values_b = (
        jnp.dot(normed, w_v, preferred_element_type=jnp.float32)
        .astype(jnp.bfloat16)
        .reshape(row_count, kv_count, HD)
    )
    scores = jnp.einsum("qkgd,tkd->kgqt", queries, keys_b, preferred_element_type=jnp.float32) * (
        1.0 / math.sqrt(HD)
    )
    causal = lax.broadcasted_iota(jnp.int32, (row_count, row_count), 0) >= lax.broadcasted_iota(
        jnp.int32, (row_count, row_count), 1
    )
    expd = jnp.where(causal, jnp.exp(scores), 0.0)
    softmax_f = expd / jnp.sum(expd, axis=-1, keepdims=True)
    softmax_b = softmax_f.astype(jnp.bfloat16)
    attended = jnp.einsum("kgqt,tkd->qkgd", softmax_b, values_b, preferred_element_type=jnp.float32)
    attended = attended.reshape(row_count, head_count * HD).astype(jnp.bfloat16)
    return (q_unit, q_inv, k_unit, k_inv, queries, keys_b, values_b, softmax_f, softmax_b, attended)


def forward_part(x_rows, norm_scale, weights, qk_gains, cos_tab, sin_tab):
    w_q, w_k, w_v, w_o = weights
    x_float, inverse, unit_row_vectors, normed = input_norm(x_rows, norm_scale)
    attended = attend_local(normed, w_q, w_k, w_v, qk_gains, cos_tab, sin_tab)[-1]
    out_part = lax.dot_general(
        attended, w_o, (((1,), (1,)), ((), ())), preferred_element_type=jnp.float32
    )
    return (x_float, out_part)


def backward_part(x_rows, cot_rows, norm_scale, weights, qk_gains, cos_tab, sin_tab):
    w_q, w_k, w_v, w_o = weights
    x_float, inverse, unit_row_vectors, normed = input_norm(x_rows, norm_scale)
    q_unit, q_inv, k_unit, k_inv, queries, keys_b, values_b, softmax_f, softmax_b, attended = (
        attend_local(normed, w_q, w_k, w_v, qk_gains, cos_tab, sin_tab)
    )
    row_count, kv_count, group_size = (queries.shape[0], queries.shape[1], queries.shape[2])
    d_attn = (
        jnp.dot(cot_rows, w_o, preferred_element_type=jnp.float32)
        .astype(jnp.bfloat16)
        .reshape(row_count, kv_count, group_size, HD)
    )
    d_probs = jnp.einsum("qkgd,tkd->kgqt", d_attn, values_b, preferred_element_type=jnp.float32)
    d_value = jnp.einsum("kgqt,qkgd->tkd", softmax_b, d_attn, preferred_element_type=jnp.float32)
    d_value = d_value.astype(jnp.bfloat16).reshape(row_count, kv_count * HD)
    d_scores = (
        softmax_f
        * (d_probs - jnp.sum(softmax_f * d_probs, axis=-1, keepdims=True))
        * (1.0 / math.sqrt(HD))
    )
    d_scores = d_scores.astype(jnp.bfloat16)
    d_query = jnp.einsum(
        "kgqt,tkd->qkgd", d_scores, keys_b, preferred_element_type=jnp.float32
    ).reshape(row_count, kv_count * group_size, HD)
    d_key = jnp.einsum("kgqt,qkgd->tkd", d_scores, queries, preferred_element_type=jnp.float32)
    d_query = rotate(d_query, cos_tab, -sin_tab)
    d_key = rotate(d_key, cos_tab, -sin_tab)
    q_term = jnp.sum(d_query * q_unit, axis=(0, 1))
    k_term = jnp.sum(d_key * k_unit, axis=(0, 1))
    q_grad = (
        unit_back(d_query * qk_gains[0], q_unit, q_inv).astype(jnp.bfloat16).reshape(row_count, -1)
    )
    k_grad = (
        unit_back(d_key * qk_gains[1], k_unit, k_inv).astype(jnp.bfloat16).reshape(row_count, -1)
    )
    contract = (((1,), (1,)), ((), ()))
    normed_part = lax.dot_general(q_grad, w_q, contract, preferred_element_type=jnp.float32)
    normed_part = normed_part + lax.dot_general(
        k_grad, w_k, contract, preferred_element_type=jnp.float32
    )
    normed_part = normed_part + lax.dot_general(
        d_value, w_v, contract, preferred_element_type=jnp.float32
    )
    columns = jnp.concatenate([q_grad, k_grad, d_value], axis=1)
    return (normed_part, unit_row_vectors, inverse, normed, columns, attended, q_term, k_term)


def tensor_sum(part):
    count = lax.axis_size("tensor")
    mine = part.astype(jnp.bfloat16)
    total = mine.astype(jnp.float32)
    for step in range(1, count):
        route = [(i, i ^ step) for i in range(count)]
        total = total + lax.ppermute(mine, "tensor", route).astype(jnp.float32)
    return total


def tensor_sums(out_part, normed_part):
    both = tensor_sum(jnp.concatenate([out_part, normed_part], axis=0))
    rows = out_part.shape[0]
    return both[:rows], both[rows:]


def run_slot(x_forward, x_backward, cot_rows, norm_scale, weights, qk_gains, cos_tab, sin_tab):
    x_float, out_part = forward_part(x_forward, norm_scale, weights, qk_gains, cos_tab, sin_tab)
    normed_part, unit_row_vectors, inverse, normed, columns, attended, q_term, k_term = (
        backward_part(x_backward, cot_rows, norm_scale, weights, qk_gains, cos_tab, sin_tab)
    )
    out_sum, d_normed = tensor_sums(out_part, normed_part)
    layer_out = (x_float + out_sum).astype(jnp.bfloat16)
    d_input = (
        cot_rows.astype(jnp.float32) + unit_back(d_normed * norm_scale, unit_row_vectors, inverse)
    ).astype(jnp.bfloat16)
    norm_term = jnp.sum(d_normed * unit_row_vectors, axis=0)
    return (layer_out, d_input, normed, columns, attended, norm_term, q_term, k_term)


def local(
    fwd_input,
    fresh_input,
    cotangent,
    fresh_cotangent,
    stash,
    norm_gain,
    qk_gain,
    w_query,
    w_key,
    w_value,
    w_out,
):
    q_width = w_query.shape[2]
    k_width = w_key.shape[2]
    left_width = q_width + 2 * k_width
    full_in, full_o = gather_weights(
        jnp.concatenate([w_query[0], w_key[0], w_value[0]], axis=1), w_out[0]
    )
    full_in = full_in.reshape(-1, left_width)
    full_o = full_o.reshape(-1, w_out.shape[2])
    weights = (
        full_in[:, :q_width],
        full_in[:, q_width : q_width + k_width],
        full_in[:, q_width + k_width :],
        full_o,
    )
    norm_scale = norm_gain[0]
    qk_gains = qk_gain[0]
    row_count = fwd_input.shape[1]
    cos_tab, sin_tab = rope_tables(row_count, HD)
    section_position_index = lax.axis_index("section")
    section_total = lax.axis_size("section")
    bit_order = list(range(section_total.bit_length() - 1))
    reloaded = stash[0]
    for bit_index in bit_order:
        reloaded = swapped(reloaded, "section", bit_index)
    first_slot = run_slot(
        fwd_input[0], reloaded[0], cotangent[0], norm_scale, weights, qk_gains, cos_tab, sin_tab
    )
    arrived = passed_along(first_slot[0], "section", 1)
    second_input = jnp.where(section_position_index == 0, fresh_input, arrived)
    returned = passed_along(first_slot[1], "section", -1)
    second_cot = jnp.where(section_position_index == section_total - 1, fresh_cotangent, returned)
    second_slot = run_slot(
        second_input, reloaded[1], second_cot, norm_scale, weights, qk_gains, cos_tab, sin_tab
    )
    out_activations = jnp.stack([first_slot[0], second_slot[0]])[None]
    grad_input = jnp.stack([first_slot[1], second_slot[1]])[None]
    grad_scale = 1.0 / math.sqrt(2 * row_count * lax.axis_size("dp"))
    normed_rows = jnp.concatenate([first_slot[2], second_slot[2]], axis=0)
    column_rows = jnp.concatenate([first_slot[3], second_slot[3]], axis=0)
    cot_rows = jnp.concatenate([cotangent[0], second_cot], axis=0)
    attended_rows = jnp.concatenate([first_slot[4], second_slot[4]], axis=0)
    contract = (((0,), (0,)), ((), ()))
    norm_term = first_slot[5] + second_slot[5]
    qk_term = jnp.stack([first_slot[6] + second_slot[6], first_slot[7] + second_slot[7]])
    feature_rows = norm_term.shape[0] // HD
    small = jnp.concatenate(
        [norm_term.reshape(feature_rows, HD), qk_term, jnp.zeros((6, HD), jnp.float32)], axis=0
    )
    gathered, sliced, smalls = exchange_grads(
        jnp.concatenate([column_rows, attended_rows], axis=1),
        jnp.stack([normed_rows, cot_rows]),
        small * grad_scale,
    )
    gathered = gathered.reshape(-1, gathered.shape[-1])
    sliced = jnp.moveaxis(sliced, 1, 0).reshape(2, -1, sliced.shape[-1])
    norm_total = jnp.sum(smalls[0, :, :feature_rows], axis=0).reshape(-1)
    qk_total = jnp.sum(smalls[:, :, feature_rows : feature_rows + 2], axis=(0, 1))
    left_term = lax.dot_general(
        sliced[0], gathered[:, :left_width], contract, preferred_element_type=jnp.float32
    )
    right_term = lax.dot_general(
        sliced[1], gathered[:, left_width:], contract, preferred_element_type=jnp.float32
    )
    left_term = left_term * grad_scale
    right_term = right_term * grad_scale
    grad_query = left_term[:, :q_width][None]
    grad_key = left_term[:, q_width : q_width + k_width][None]
    grad_value = left_term[:, q_width + k_width :][None]
    grad_out = right_term[None]
    return (
        out_activations,
        grad_input,
        grad_query,
        grad_key,
        grad_value,
        grad_out,
        norm_total[None],
        qk_total[None],
    )


def solution(mesh):
    return jax.shard_map(
        local,
        mesh=mesh,
        in_specs=(
            P("section", "dp", None),
            P("dp", None),
            P("section", "dp", None),
            P("dp", None),
            P("section", None, "dp", None),
            P("section", None),
            P("section", None, None),
            P("section", "dp", "tensor"),
            P("section", "dp", "tensor"),
            P("section", "dp", "tensor"),
            P("section", "dp", "tensor"),
        ),
        out_specs=(
            P("section", None, "dp", None),
            P("section", None, "dp", None),
            P("section", "dp", "tensor"),
            P("section", "dp", "tensor"),
            P("section", "dp", "tensor"),
            P("section", "dp", "tensor"),
            P("section", None),
            P("section", None, None),
        ),
        check_vma=False,
    )
```

```python
import functools
import math

import jax
import jax.numpy as jnp
from jax import lax
from jax.experimental import pallas as pl
from jax.experimental.pallas import tpu as pltpu
from jax.sharding import PartitionSpec as P

HD = 128


EPSILON = 1e-06
THETA = 1000000.0


def swapped(block, axis, apart):
    count = lax.axis_size(axis)
    route = []
    for low in range(count):
        high = low | 1 << apart
        if high != low and high < count:
            route += [(low, high), (high, low)]
    return lax.ppermute(block, axis, route)


def passed_along(array, axis, by):
    count = lax.axis_size(axis)
    pairs = [(i, i + by) for i in range(count) if 0 <= i + by < count]
    return lax.ppermute(array, axis, pairs)


def grid_of(count):
    tall = 4 if count % 4 == 0 else 1
    return tall, count // tall


def meet(peers):
    barrier = pltpu.get_barrier_semaphore()
    for peer in peers:
        pl.semaphore_signal(barrier, inc=1, device_id=peer)
    pl.semaphore_wait(barrier, len(peers))


class Sends:
    def __init__(self, sems):
        self.sems = sems
        self.started = []

    def start(self, src, dst, recv, peer):
        copy = pltpu.make_async_remote_copy(
            src_ref=src,
            dst_ref=dst,
            send_sem=self.sems.at[len(self.started)],
            recv_sem=recv,
            device_id=peer,
        )
        copy.start()
        self.started.append(copy)

    def arrived(self, dst, recv, peer):
        pltpu.make_async_remote_copy(
            src_ref=dst, dst_ref=dst, send_sem=self.sems.at[0], recv_sem=recv, device_id=peer
        ).wait_recv()

    def finish(self):
        for copy in self.started:
            copy.wait_send()


def neighbours(count):
    tall, wide = grid_of(count)
    me = lax.axis_index("dp")
    row, col = me // wide, me % wide
    across = [row * wide + (col + i) % wide for i in range(1, wide)]
    along = [((row + i) % tall) * wide + col for i in range(1, tall)]
    return me, row, across, along


def spread(sends, pieces, me, across, along, recv):
    for c, (src, dst) in enumerate(pieces):
        for peer in along + across:
            sends.start(src, dst(me), recv.at[me, c], {"dp": peer})


def relay(sends, pieces, c, across, along, recv):
    dst = pieces[c][1]
    for peer in along:
        sends.arrived(dst(peer), recv.at[peer, c], {"dp": peer})
        for other in across:
            sends.start(dst(peer), dst(peer), recv.at[peer, c], {"dp": other})


def collect(sends, pieces, c, row, count, across, recv):
    tall, wide = grid_of(count)
    dst = pieces[c][1]
    for other in across:
        for i in range(tall):
            shard = ((row + i) % tall) * wide + other % wide
            sends.arrived(dst(shard), recv.at[shard, c], {"dp": other})


def halves(src, full, depth):
    half = depth // 2
    return [
        (src.at[pl.ds(i * half, half)], lambda j, i=i: full.at[j, pl.ds(i * half, half)])
        for i in range(2)
    ]


def weights_kernel(count, in_ref, out_ref, full_in, full_out, send, recv, own):
    me, row, across, along = neighbours(count)
    depth = in_ref.shape[0]
    meet([{"dp": j} for j in along + across])
    pieces = halves(in_ref, full_in, depth) + halves(out_ref, full_out, depth)
    sends = Sends(send)
    spread(sends, pieces, me, across, along, recv)
    mine = [
        pltpu.make_async_copy(in_ref, full_in.at[me], own.at[0]),
        pltpu.make_async_copy(out_ref, full_out.at[me], own.at[1]),
    ]
    for copy in mine:
        copy.start()
    for c in range(len(pieces)):
        relay(sends, pieces, c, across, along, recv)
    for c in range(len(pieces)):
        collect(sends, pieces, c, row, count, across, recv)
    for copy in mine:
        copy.wait()
    sends.finish()


def grads_kernel(
    count, cols_a, cols_b, acts_a, acts_b, small_ref, full, sliced, smalls, send, recv, own
):
    me, row, across, along = neighbours(count)
    core = lax.axis_index("tensor")
    depth = sliced.shape[-1]
    everyone = [{"dp": (me + i) % count} for i in range(1, count)]
    crossed = [{"dp": (me + i) % count, "tensor": 1 - core} for i in range(count)]
    meet(everyone + crossed)
    pieces = [(cols_a, lambda j: full.at[j, 0]), (cols_b, lambda j: full.at[j, 1])]
    acts = (acts_a, acts_b)
    sends = Sends(send)
    spread(sends, pieces, me, across, along, recv)
    for peer in everyone:
        block = pl.ds(pl.multiple_of(peer["dp"] * depth, depth), depth)
        for i in range(2):
            sends.start(acts[i].at[:, :, block], sliced.at[me, i], recv.at[me, 5 + i], peer)
    for peer in everyone + crossed:
        sends.start(small_ref, smalls.at[core, me], recv.at[me, 3 + core], peer)
    block = pl.ds(pl.multiple_of(me * depth, depth), depth)
    mine = [
        pltpu.make_async_copy(cols_a, full.at[me, 0], own.at[0]),
        pltpu.make_async_copy(cols_b, full.at[me, 1], own.at[1]),
        pltpu.make_async_copy(acts_a.at[:, :, block], sliced.at[me, 0], own.at[3]),
        pltpu.make_async_copy(acts_b.at[:, :, block], sliced.at[me, 1], own.at[4]),
        pltpu.make_async_copy(small_ref, smalls.at[core, me], own.at[2]),
    ]
    for copy in mine:
        copy.start()
    for c in range(2):
        relay(sends, pieces, c, across, along, recv)
    for c in range(2):
        collect(sends, pieces, c, row, count, across, recv)
    for peer in everyone:
        j = peer["dp"]
        for i in range(2):
            sends.arrived(sliced.at[j, i], recv.at[j, 5 + i], peer)
        sends.arrived(smalls.at[core, j], recv.at[j, 3 + core], peer)
    for peer in crossed:
        j = peer["dp"]
        sends.arrived(smalls.at[1 - core, j], recv.at[j, 4 - core], peer)
    for copy in mine:
        copy.wait()
    sends.finish()


ANY = pl.BlockSpec(memory_space=pl.ANY)


def gather_weights(w_in, w_out):
    count = lax.axis_size("dp")
    tall, wide = grid_of(count)
    sent = 4 * (tall + wide - 2 + (tall - 1) * (wide - 1))
    return pl.pallas_call(
        functools.partial(weights_kernel, count),
        out_shape=[jax.ShapeDtypeStruct((count,) + w.shape, w.dtype) for w in (w_in, w_out)],
        in_specs=[ANY] * 2,
        out_specs=[ANY] * 2,
        scratch_shapes=[
            pltpu.SemaphoreType.DMA((sent,)),
            pltpu.SemaphoreType.DMA((count, 4)),
            pltpu.SemaphoreType.DMA((2,)),
        ],
        compiler_params=pltpu.CompilerParams(collective_id=0, has_side_effects=True),
    )(w_in, w_out)


def exchange_grads(cols, cols_b, acts, acts_b, small):
    count = lax.axis_size("dp")
    tall, wide = grid_of(count)
    rows, width = acts.shape[1:]
    sent = 2 * (tall + wide - 2 + (tall - 1) * (wide - 1)) + 4 * count - 3
    return pl.pallas_call(
        functools.partial(grads_kernel, count),
        out_shape=[
            jax.ShapeDtypeStruct((count, 2) + cols.shape, cols.dtype),
            jax.ShapeDtypeStruct((count, 2, 2, rows, width // count), acts.dtype),
            jax.ShapeDtypeStruct((2, count) + small.shape, small.dtype),
        ],
        in_specs=[ANY] * 5,
        out_specs=[ANY] * 3,
        scratch_shapes=[
            pltpu.SemaphoreType.DMA((sent,)),
            pltpu.SemaphoreType.DMA((count, 7)),
            pltpu.SemaphoreType.DMA((5,)),
        ],
        compiler_params=pltpu.CompilerParams(collective_id=1, has_side_effects=True),
    )(cols, cols_b, acts, acts_b, small)


def rope_tables(length, width):
    half_width = width // 2
    freqs = jnp.exp(jnp.arange(half_width, dtype=jnp.float32) * (-2.0 * math.log(THETA) / width))
    angles = jnp.arange(length, dtype=jnp.float32)[:, None] * freqs[None, :]
    return (jnp.cos(angles), jnp.sin(angles))


def nt(left, right):
    return lax.dot_general(
        left, right, (((1,), (1,)), ((), ())), preferred_element_type=jnp.float32
    )


def tn(left, right):
    return lax.dot_general(
        left, right, (((0,), (0,)), ((), ())), preferred_element_type=jnp.float32
    )


def nn(left, right):
    return jnp.dot(left, right, preferred_element_type=jnp.float32)


def turn(vectors, tables, sign):
    cos_tab = tables[0, : vectors.shape[0]]
    sin_tab = tables[1, : vectors.shape[0]]
    return vectors * cos_tab + pltpu.roll(vectors, HD // 2, 1) * (sign * sin_tab)


def head_norm(raw_heads):
    inverse = lax.rsqrt(jnp.mean(raw_heads * raw_heads, axis=-1, keepdims=True) + EPSILON)
    return (raw_heads * inverse, inverse)


def unit_back(grad_unit, unit_row_vectors, inverse):
    return inverse * (
        grad_unit
        - unit_row_vectors * jnp.mean(grad_unit * unit_row_vectors, axis=-1, keepdims=True)
    )


def tall_heads(wide):
    return jnp.concatenate(
        [wide[:, h * HD : (h + 1) * HD] for h in range(wide.shape[1] // HD)], axis=0
    )


def wide_heads(tall, rows):
    return jnp.concatenate(
        [tall[h * rows : (h + 1) * rows] for h in range(tall.shape[0] // rows)], axis=1
    )


def lower(tall, rows):
    return jnp.concatenate(
        [tall[h + rows : h + 2 * rows] for h in range(0, tall.shape[0], 2 * rows)], axis=0
    )


def slot_kernel(
    xf_ref, xb_ref, g_ref, gain_ref, qk_ref, tables, wi_ref, wo_ref,
    parts_ref, cols_ref, acts_ref, terms_ref,
):
    rows = xf_ref.shape[0]
    q_width = wo_ref.shape[1]
    scale = 1.0 / math.sqrt(HD)
    q_gain, k_gain = qk_ref[0:1], qk_ref[1:2]
    x = jnp.concatenate([xf_ref[...], xb_ref[...]], axis=0).astype(jnp.float32)
    unit, _ = head_norm(x)
    normed = (unit * gain_ref[...]).astype(jnp.bfloat16)
    acts_ref[0] = normed[rows:]
    acts_ref[1] = g_ref[...]
    qkv = nn(normed, wi_ref[...])
    q_unit, q_inv = head_norm(tall_heads(qkv[:, :q_width]))
    k_unit, k_inv = head_norm(qkv[:, q_width : q_width + HD])
    values = qkv[:, q_width + HD :].astype(jnp.bfloat16)
    queries = turn(q_unit * q_gain, tables, 1.0).astype(jnp.bfloat16)
    keys = turn(k_unit * k_gain, tables, 1.0).astype(jnp.bfloat16)
    scores = nt(queries, keys) * scale
    row = lax.rem(lax.broadcasted_iota(jnp.int32, scores.shape, 0), 2 * rows)
    col = lax.broadcasted_iota(jnp.int32, scores.shape, 1)
    seen = (row >= col) & ((row < rows) | (col >= rows))
    expd = jnp.where(seen, jnp.exp(scores), 0.0)
    probs = expd / jnp.sum(expd, axis=-1, keepdims=True)
    probs_b = probs.astype(jnp.bfloat16)
    attended = wide_heads(nn(probs_b, values), 2 * rows).astype(jnp.bfloat16)
    parts_ref[:rows] = nt(attended[:rows], wo_ref[...]).astype(jnp.bfloat16)
    d_attn = tall_heads(nn(g_ref[...], wo_ref[...])).astype(jnp.bfloat16)
    probs, q_unit, q_inv = lower(probs, rows), lower(q_unit, rows), lower(q_inv, rows)
    probs_b, queries = lower(probs_b, rows), lower(queries, rows)
    d_probs = nt(d_attn, values)
    d_scores = probs * (d_probs - jnp.sum(probs * d_probs, axis=-1, keepdims=True)) * scale
    d_scores = d_scores.astype(jnp.bfloat16)
    d_value = tn(probs_b, d_attn)[rows:].astype(jnp.bfloat16)
    d_query = turn(nn(d_scores, keys), tables, -1.0)
    d_key = turn(tn(d_scores, queries)[rows:], tables, -1.0)
    k_unit, k_inv = k_unit[rows:], k_inv[rows:]
    terms_ref[0:1] = jnp.sum(d_query * q_unit, axis=0, keepdims=True)
    terms_ref[1:2] = jnp.sum(d_key * k_unit, axis=0, keepdims=True)
    q_grad = wide_heads(unit_back(d_query * q_gain, q_unit, q_inv), rows).astype(jnp.bfloat16)
    k_grad = unit_back(d_key * k_gain, k_unit, k_inv).astype(jnp.bfloat16)
    columns = jnp.concatenate([q_grad, k_grad, d_value], axis=1)
    cols_ref[:, : columns.shape[1]] = columns
    cols_ref[:, columns.shape[1] :] = attended[rows:]
    parts_ref[rows:] = nt(columns, wi_ref[...]).astype(jnp.bfloat16)


def finish_kernel(xf_ref, xb_ref, g_ref, gain_ref, mine_ref, other_ref, out_ref, back_ref, term_ref):
    rows = xf_ref.shape[0]
    total = mine_ref[...].astype(jnp.float32) + other_ref[...].astype(jnp.float32)
    out_ref[...] = (xf_ref[...].astype(jnp.float32) + total[:rows]).astype(jnp.bfloat16)
    unit, inverse = head_norm(xb_ref[...].astype(jnp.float32))
    d_normed = total[rows:]
    d_input = g_ref[...].astype(jnp.float32) + unit_back(d_normed * gain_ref[...], unit, inverse)
    back_ref[...] = d_input.astype(jnp.bfloat16)
    term_ref[...] = jnp.sum(d_normed * unit, axis=0, keepdims=True)


ROOM = pltpu.CompilerParams(vmem_limit_bytes=48 * 1024 * 1024)


def run_slot(x_forward, x_backward, cot_rows, norm_scale, weights, qk_gains, tables):
    rows, width = x_forward.shape
    w_in, w_out = weights
    shape = jax.ShapeDtypeStruct
    parts, cols, acts, terms = pl.pallas_call(
        slot_kernel,
        out_shape=[
            shape((2 * rows, width), jnp.bfloat16),
            shape((rows, w_in.shape[1] + w_out.shape[1]), jnp.bfloat16),
            shape((2, rows, width), jnp.bfloat16),
            shape((2, HD), jnp.float32),
        ],
        compiler_params=ROOM,
    )(x_forward, x_backward, cot_rows, norm_scale, qk_gains, tables, w_in, w_out)
    other = lax.ppermute(parts, "tensor", [(0, 1), (1, 0)])
    layer_out, d_input, norm_term = pl.pallas_call(
        finish_kernel,
        out_shape=[
            shape((rows, width), jnp.bfloat16),
            shape((rows, width), jnp.bfloat16),
            shape((1, width), jnp.float32),
        ],
        compiler_params=ROOM,
    )(x_forward, x_backward, cot_rows, norm_scale, parts, other)
    return layer_out, d_input, cols, acts, norm_term, terms


def local(
    fwd_input,
    fresh_input,
    cotangent,
    fresh_cotangent,
    stash,
    norm_gain,
    qk_gain,
    w_query,
    w_key,
    w_value,
    w_out,
):
    q_width = w_query.shape[2]
    k_width = w_key.shape[2]
    left_width = q_width + 2 * k_width
    full_in, full_o = gather_weights(
        jnp.concatenate([w_query[0], w_key[0], w_value[0]], axis=1), w_out[0]
    )
    full_in = full_in.reshape(-1, left_width)
    full_o = full_o.reshape(-1, w_out.shape[2])
    weights = (full_in, full_o)
    norm_scale = norm_gain
    qk_gains = qk_gain[0]
    row_count = fwd_input.shape[1]
    cos_tab, sin_tab = rope_tables(row_count, HD)
    tables = jnp.stack(
        [
            jnp.concatenate([cos_tab, cos_tab], axis=1),
            jnp.concatenate([-sin_tab, sin_tab], axis=1),
        ]
    )
    tables = jnp.tile(tables, (1, 2 * q_width // HD, 1))
    section_position_index = lax.axis_index("section")
    section_total = lax.axis_size("section")
    bit_order = list(range(section_total.bit_length() - 1))
    reloaded = stash[0]
    for bit_index in bit_order:
        reloaded = swapped(reloaded, "section", bit_index)
    first_slot = run_slot(
        fwd_input[0], reloaded[0], cotangent[0], norm_scale, weights, qk_gains, tables
    )
    arrived = passed_along(first_slot[0], "section", 1)
    second_input = jnp.where(section_position_index == 0, fresh_input, arrived)
    returned = passed_along(first_slot[1], "section", -1)
    second_cot = jnp.where(section_position_index == section_total - 1, fresh_cotangent, returned)
    second_slot = run_slot(
        second_input, reloaded[1], second_cot, norm_scale, weights, qk_gains, tables
    )
    out_activations = jnp.stack([first_slot[0], second_slot[0]])[None]
    grad_input = jnp.stack([first_slot[1], second_slot[1]])[None]
    grad_scale = 1.0 / math.sqrt(2 * row_count * lax.axis_size("dp"))
    contract = (((0,), (0,)), ((), ()))
    norm_term = first_slot[4] + second_slot[4]
    qk_term = first_slot[5] + second_slot[5]
    feature_rows = norm_term.shape[1] // HD
    small = jnp.concatenate(
        [norm_term.reshape(feature_rows, HD), qk_term, jnp.zeros((6, HD), jnp.float32)], axis=0
    )
    gathered, sliced, smalls = exchange_grads(
        first_slot[2], second_slot[2], first_slot[3], second_slot[3], small * grad_scale
    )
    gathered = gathered.reshape(-1, gathered.shape[-1])
    sliced = jnp.moveaxis(sliced, 2, 0).reshape(2, -1, sliced.shape[-1])
    norm_total = jnp.sum(smalls[0, :, :feature_rows], axis=0).reshape(-1)
    qk_total = jnp.sum(smalls[:, :, feature_rows : feature_rows + 2], axis=(0, 1))
    left_term = lax.dot_general(
        sliced[0], gathered[:, :left_width], contract, preferred_element_type=jnp.float32
    )
    right_term = lax.dot_general(
        sliced[1], gathered[:, left_width:], contract, preferred_element_type=jnp.float32
    )
    left_term = left_term * grad_scale
    right_term = right_term * grad_scale
    grad_query = left_term[:, :q_width][None]
    grad_key = left_term[:, q_width : q_width + k_width][None]
    grad_value = left_term[:, q_width + k_width :][None]
    grad_out = right_term[None]
    return (
        out_activations,
        grad_input,
        grad_query,
        grad_key,
        grad_value,
        grad_out,
        norm_total[None],
        qk_total[None],
    )


def solution(mesh):
    return jax.shard_map(
        local,
        mesh=mesh,
        in_specs=(
            P("section", "dp", None),
            P("dp", None),
            P("section", "dp", None),
            P("dp", None),
            P("section", None, "dp", None),
            P("section", None),
            P("section", None, None),
            P("section", "dp", "tensor"),
            P("section", "dp", "tensor"),
            P("section", "dp", "tensor"),
            P("section", "dp", "tensor"),
        ),
        out_specs=(
            P("section", None, "dp", None),
            P("section", None, "dp", None),
            P("section", "dp", "tensor"),
            P("section", "dp", "tensor"),
            P("section", "dp", "tensor"),
            P("section", "dp", "tensor"),
            P("section", None),
            P("section", None, None),
        ),
        check_vma=False,
    )
```

```python
import functools
import math

import jax
import jax.numpy as jnp
from jax import lax
from jax.experimental import pallas as pl
from jax.experimental.pallas import tpu as pltpu
from jax.sharding import PartitionSpec as P

HD = 128


EPSILON = 1e-06
THETA = 1000000.0


def swapped(block, axis, apart):
    count = lax.axis_size(axis)
    route = []
    for low in range(count):
        high = low | 1 << apart
        if high != low and high < count:
            route += [(low, high), (high, low)]
    return lax.ppermute(block, axis, route)


def passed_along(array, axis, by):
    count = lax.axis_size(axis)
    pairs = [(i, i + by) for i in range(count) if 0 <= i + by < count]
    return lax.ppermute(array, axis, pairs)


def grid_of(count):
    tall = 4 if count % 4 == 0 else 1
    return tall, count // tall


def meet(peers):
    barrier = pltpu.get_barrier_semaphore()
    for peer in peers:
        pl.semaphore_signal(barrier, inc=1, device_id=peer)
    pl.semaphore_wait(barrier, len(peers))


class Sends:
    def __init__(self, sems):
        self.sems = sems
        self.started = []

    def start(self, src, dst, recv, peer, cond=None):
        copy = pltpu.make_async_remote_copy(
            src_ref=src,
            dst_ref=dst,
            send_sem=self.sems.at[len(self.started)],
            recv_sem=recv,
            device_id=peer,
        )
        if cond is None:
            copy.start()
        else:
            pl.when(cond)(copy.start)
        self.started.append((cond, copy))

    def arrived(self, dst, recv, peer):
        pltpu.make_async_remote_copy(
            src_ref=dst, dst_ref=dst, send_sem=self.sems.at[0], recv_sem=recv, device_id=peer
        ).wait_recv()

    def finish(self):
        for cond, copy in self.started:
            if cond is None:
                copy.wait_send()
            else:
                pl.when(cond)(copy.wait_send)


def relayed(count, pieces, early):
    tall, wide = grid_of(count)
    plain = wide + 1 + (tall - 1) * 2 * wide
    first = wide + 1 + 2 * (wide - 1) + (tall - 1) * 2 * wide
    return (pieces - early) * plain + early * first


def neighbours(count):
    tall, wide = grid_of(count)
    me = lax.axis_index("dp")
    row, col = me // wide, me % wide
    across = [row * wide + (col + i) % wide for i in range(1, wide)]
    along = [((row + i) % tall) * wide + col for i in range(1, tall)]
    return me, row, across, along


def cut(src, full, depth, parts):
    part = depth // parts
    return [
        (src.at[pl.ds(i * part, part)], lambda j, i=i: full.at[j, pl.ds(i * part, part)])
        for i in range(parts)
    ]


class Relay:
    def __init__(self, count, pieces, early, sends, recv):
        self.tall, self.wide = grid_of(count)
        self.me, self.row, self.across, self.along = neighbours(count)
        self.pieces, self.early, self.sends, self.recv = pieces, early, sends, recv
        self.up, self.down = self.row < self.tall - 1, self.row > 0

    def pass_on(self, cond, c, shard, peer, own=False):
        src, dst = self.pieces[c]
        src = src if own else dst(shard)
        self.sends.start(src, dst(shard), self.recv.at[shard, c], {"dp": peer}, cond)

    def begin(self, chosen):
        for c in chosen:
            for peer in self.across:
                self.pass_on(None, c, self.me, peer, True)
            self.pass_on(self.up, c, self.me, self.me + self.wide, True)
            self.pass_on(self.down, c, self.me, self.me - self.wide, True)

    def take(self, cond, c, shard):
        arrive = functools.partial(
            self.sends.arrived, self.pieces[c][1](shard), self.recv.at[shard, c], {"dp": self.me}
        )
        if cond is None:
            arrive()
        else:
            pl.when(cond)(arrive)

    def hop(self, c, d):
        wide, me = self.wide, self.me
        shifts = [0] + [p - me for p in self.across] if c in self.early else [0]
        if d == 1:
            for shift in shifts[1:]:
                self.take(None, c, me + shift)
                self.pass_on(self.up, c, me + shift, me + wide)
                self.pass_on(self.down, c, me + shift, me - wide)
        for shift in shifts:
            for near, here, on, after in (
                (me - d * wide, self.row >= d, self.up, me + wide),
                (me + d * wide, self.row + d < self.tall, self.down, me - wide),
            ):
                self.take(here, c, near + shift)
                self.pass_on(here & on, c, near + shift, after)
                if c not in self.early:
                    for peer in self.across:
                        self.pass_on(here, c, near, peer)

    def run(self, chosen):
        for wave in range(len(chosen) + self.tall - 2):
            for d in range(1, self.tall):
                if 0 <= wave - d + 1 < len(chosen):
                    self.hop(chosen[wave - d + 1], d)

    def end(self, chosen):
        for c in chosen:
            if c in self.early:
                continue
            for other in self.across:
                for i in range(self.tall):
                    self.take(None, c, ((self.row + i) % self.tall) * self.wide + other % self.wide)


def weights_kernel(count, in_ref, out_ref, full_in, full_out, send, recv, own):
    me, row, across, along = neighbours(count)
    depth = in_ref.shape[0]
    meet([{"dp": j} for j in along + across])
    sends = Sends(send)
    pieces = cut(in_ref, full_in, depth, 4) + cut(out_ref, full_out, depth, 4)
    relay = Relay(count, pieces, (0,), sends, recv)
    order = list(range(8))
    relay.begin(order)
    mine = [
        pltpu.make_async_copy(in_ref, full_in.at[me], own.at[0]),
        pltpu.make_async_copy(out_ref, full_out.at[me], own.at[1]),
    ]
    for copy in mine:
        copy.start()
    relay.run(order)
    relay.end(order)
    for copy in mine:
        copy.wait()
    sends.finish()


def grads_kernel(
    count, cols_a, cols_b, acts_a, acts_b, small_ref, full, sliced, smalls, send, recv, own
):
    me, row, across, along = neighbours(count)
    core = lax.axis_index("tensor")
    depth = sliced.shape[-1]
    everyone = [{"dp": (me + i) % count} for i in range(1, count)]
    crossed = [{"dp": (me + i) % count, "tensor": 1 - core} for i in range(count)]
    meet(everyone + crossed)
    half = cols_a.shape[0] // 2
    pieces = [
        (cols.at[pl.ds(p * half, half)], lambda j, i=i, p=p: full.at[j, i, pl.ds(p * half, half)])
        for i, cols in enumerate((cols_a, cols_b))
        for p in range(2)
    ]
    acts = (acts_a, acts_b)
    sends = Sends(send)
    relay = Relay(count, pieces, (), sends, recv)
    relay.begin(range(4))
    for peer in everyone:
        block = pl.ds(pl.multiple_of(peer["dp"] * depth, depth), depth)
        for i in range(2):
            sends.start(acts[i].at[:, :, block], sliced.at[me, i], recv.at[me, 6 + i], peer)
    for peer in everyone + crossed:
        sends.start(small_ref, smalls.at[core, me], recv.at[me, 4 + core], peer)
    block = pl.ds(pl.multiple_of(me * depth, depth), depth)
    mine = [
        pltpu.make_async_copy(cols_a, full.at[me, 0], own.at[0]),
        pltpu.make_async_copy(cols_b, full.at[me, 1], own.at[1]),
        pltpu.make_async_copy(acts_a.at[:, :, block], sliced.at[me, 0], own.at[3]),
        pltpu.make_async_copy(acts_b.at[:, :, block], sliced.at[me, 1], own.at[4]),
        pltpu.make_async_copy(small_ref, smalls.at[core, me], own.at[2]),
    ]
    for copy in mine:
        copy.start()
    relay.run(range(4))
    relay.end(range(4))
    for peer in everyone:
        j = peer["dp"]
        for i in range(2):
            sends.arrived(sliced.at[j, i], recv.at[j, 6 + i], peer)
        sends.arrived(smalls.at[core, j], recv.at[j, 4 + core], peer)
    for peer in crossed:
        j = peer["dp"]
        sends.arrived(smalls.at[1 - core, j], recv.at[j, 5 - core], peer)
    for copy in mine:
        copy.wait()
    sends.finish()


ANY = pl.BlockSpec(memory_space=pl.ANY)


def gather_weights(w_in, w_out):
    count = lax.axis_size("dp")
    sent = relayed(count, 8, 1)
    return pl.pallas_call(
        functools.partial(weights_kernel, count),
        out_shape=[jax.ShapeDtypeStruct((count,) + w.shape, w.dtype) for w in (w_in, w_out)],
        in_specs=[ANY] * 2,
        out_specs=[ANY] * 2,
        scratch_shapes=[
            pltpu.SemaphoreType.DMA((sent,)),
            pltpu.SemaphoreType.DMA((count, 8)),
            pltpu.SemaphoreType.DMA((2,)),
        ],
        compiler_params=pltpu.CompilerParams(collective_id=0, has_side_effects=True),
    )(w_in, w_out)


def exchange_grads(cols, cols_b, acts, acts_b, small):
    count = lax.axis_size("dp")
    rows, width = acts.shape[1:]
    sent = relayed(count, 4, 0) + 4 * count - 3
    return pl.pallas_call(
        functools.partial(grads_kernel, count),
        out_shape=[
            jax.ShapeDtypeStruct((count, 2) + cols.shape, cols.dtype),
            jax.ShapeDtypeStruct((count, 2, 2, rows, width // count), acts.dtype),
            jax.ShapeDtypeStruct((2, count) + small.shape, small.dtype),
        ],
        in_specs=[ANY] * 5,
        out_specs=[ANY] * 3,
        scratch_shapes=[
            pltpu.SemaphoreType.DMA((sent,)),
            pltpu.SemaphoreType.DMA((count, 8)),
            pltpu.SemaphoreType.DMA((5,)),
        ],
        compiler_params=pltpu.CompilerParams(collective_id=1, has_side_effects=True),
    )(cols, cols_b, acts, acts_b, small)


def rope_tables(length, width):
    half_width = width // 2
    freqs = jnp.exp(jnp.arange(half_width, dtype=jnp.float32) * (-2.0 * math.log(THETA) / width))
    angles = jnp.arange(length, dtype=jnp.float32)[:, None] * freqs[None, :]
    return (jnp.cos(angles), jnp.sin(angles))


def nt(left, right):
    return lax.dot_general(
        left, right, (((1,), (1,)), ((), ())), preferred_element_type=jnp.float32
    )


def tn(left, right):
    return lax.dot_general(
        left, right, (((0,), (0,)), ((), ())), preferred_element_type=jnp.float32
    )


def nn(left, right):
    return jnp.dot(left, right, preferred_element_type=jnp.float32)


def turn(vectors, tables, sign):
    cos_tab = tables[0, : vectors.shape[0]]
    sin_tab = tables[1, : vectors.shape[0]]
    return vectors * cos_tab + pltpu.roll(vectors, HD // 2, 1) * (sign * sin_tab)


def head_norm(raw_heads):
    inverse = lax.rsqrt(jnp.mean(raw_heads * raw_heads, axis=-1, keepdims=True) + EPSILON)
    return (raw_heads * inverse, inverse)


def unit_back(grad_unit, unit_row_vectors, inverse):
    return inverse * (
        grad_unit
        - unit_row_vectors * jnp.mean(grad_unit * unit_row_vectors, axis=-1, keepdims=True)
    )


def tall_heads(wide):
    return jnp.concatenate(
        [wide[:, h * HD : (h + 1) * HD] for h in range(wide.shape[1] // HD)], axis=0
    )


def wide_heads(tall, rows):
    return jnp.concatenate(
        [tall[h * rows : (h + 1) * rows] for h in range(tall.shape[0] // rows)], axis=1
    )


def lower(tall, rows):
    return jnp.concatenate(
        [tall[h + rows : h + 2 * rows] for h in range(0, tall.shape[0], 2 * rows)], axis=0
    )


def slot_kernel(
    xf_ref, xb_ref, g_ref, gain_ref, qk_ref, tables, wi_ref, wo_ref,
    parts_ref, cols_ref, acts_ref, terms_ref,
):
    rows = xf_ref.shape[0]
    q_width = wo_ref.shape[1]
    scale = 1.0 / math.sqrt(HD)
    q_gain, k_gain = qk_ref[0:1], qk_ref[1:2]
    x = jnp.concatenate([xf_ref[...], xb_ref[...]], axis=0).astype(jnp.float32)
    unit, _ = head_norm(x)
    normed = (unit * gain_ref[...]).astype(jnp.bfloat16)
    acts_ref[0] = normed[rows:]
    acts_ref[1] = g_ref[...]
    qkv = nn(normed, wi_ref[...])
    q_unit, q_inv = head_norm(tall_heads(qkv[:, :q_width]))
    k_unit, k_inv = head_norm(qkv[:, q_width : q_width + HD])
    values = qkv[:, q_width + HD :].astype(jnp.bfloat16)
    queries = turn(q_unit * q_gain, tables, 1.0).astype(jnp.bfloat16)
    keys = turn(k_unit * k_gain, tables, 1.0).astype(jnp.bfloat16)
    scores = nt(queries, keys) * scale
    row = lax.rem(lax.broadcasted_iota(jnp.int32, scores.shape, 0), 2 * rows)
    col = lax.broadcasted_iota(jnp.int32, scores.shape, 1)
    seen = (row >= col) & ((row < rows) | (col >= rows))
    expd = jnp.where(seen, jnp.exp(scores), 0.0)
    probs = expd / jnp.sum(expd, axis=-1, keepdims=True)
    probs_b = probs.astype(jnp.bfloat16)
    attended = wide_heads(nn(probs_b, values), 2 * rows).astype(jnp.bfloat16)
    parts_ref[:rows] = nt(attended[:rows], wo_ref[...]).astype(jnp.bfloat16)
    d_attn = tall_heads(nn(g_ref[...], wo_ref[...])).astype(jnp.bfloat16)
    probs, q_unit, q_inv = lower(probs, rows), lower(q_unit, rows), lower(q_inv, rows)
    probs_b, queries = lower(probs_b, rows), lower(queries, rows)
    d_probs = nt(d_attn, values)
    d_scores = probs * (d_probs - jnp.sum(probs * d_probs, axis=-1, keepdims=True)) * scale
    d_scores = d_scores.astype(jnp.bfloat16)
    d_value = tn(probs_b, d_attn)[rows:].astype(jnp.bfloat16)
    d_query = turn(nn(d_scores, keys), tables, -1.0)
    d_key = turn(tn(d_scores, queries)[rows:], tables, -1.0)
    k_unit, k_inv = k_unit[rows:], k_inv[rows:]
    terms_ref[0:1] = jnp.sum(d_query * q_unit, axis=0, keepdims=True)
    terms_ref[1:2] = jnp.sum(d_key * k_unit, axis=0, keepdims=True)
    q_grad = wide_heads(unit_back(d_query * q_gain, q_unit, q_inv), rows).astype(jnp.bfloat16)
    k_grad = unit_back(d_key * k_gain, k_unit, k_inv).astype(jnp.bfloat16)
    columns = jnp.concatenate([q_grad, k_grad, d_value], axis=1)
    cols_ref[:, : columns.shape[1]] = columns
    cols_ref[:, columns.shape[1] :] = attended[rows:]
    parts_ref[rows:] = nt(columns, wi_ref[...]).astype(jnp.bfloat16)


def finish_kernel(xf_ref, xb_ref, g_ref, gain_ref, mine_ref, other_ref, out_ref, back_ref, term_ref):
    rows = xf_ref.shape[0]
    total = mine_ref[...].astype(jnp.float32) + other_ref[...].astype(jnp.float32)
    out_ref[...] = (xf_ref[...].astype(jnp.float32) + total[:rows]).astype(jnp.bfloat16)
    unit, inverse = head_norm(xb_ref[...].astype(jnp.float32))
    d_normed = total[rows:]
    d_input = g_ref[...].astype(jnp.float32) + unit_back(d_normed * gain_ref[...], unit, inverse)
    back_ref[...] = d_input.astype(jnp.bfloat16)
    term_ref[...] = jnp.sum(d_normed * unit, axis=0, keepdims=True)


ROOM = pltpu.CompilerParams(vmem_limit_bytes=48 * 1024 * 1024)


def run_slot(x_forward, x_backward, cot_rows, norm_scale, weights, qk_gains, tables):
    rows, width = x_forward.shape
    w_in, w_out = weights
    shape = jax.ShapeDtypeStruct
    parts, cols, acts, terms = pl.pallas_call(
        slot_kernel,
        out_shape=[
            shape((2 * rows, width), jnp.bfloat16),
            shape((rows, w_in.shape[1] + w_out.shape[1]), jnp.bfloat16),
            shape((2, rows, width), jnp.bfloat16),
            shape((2, HD), jnp.float32),
        ],
        compiler_params=ROOM,
    )(x_forward, x_backward, cot_rows, norm_scale, qk_gains, tables, w_in, w_out)
    other = lax.ppermute(parts, "tensor", [(0, 1), (1, 0)])
    layer_out, d_input, norm_term = pl.pallas_call(
        finish_kernel,
        out_shape=[
            shape((rows, width), jnp.bfloat16),
            shape((rows, width), jnp.bfloat16),
            shape((1, width), jnp.float32),
        ],
        compiler_params=ROOM,
    )(x_forward, x_backward, cot_rows, norm_scale, parts, other)
    return layer_out, d_input, cols, acts, norm_term, terms


def local(
    fwd_input,
    fresh_input,
    cotangent,
    fresh_cotangent,
    stash,
    norm_gain,
    qk_gain,
    w_query,
    w_key,
    w_value,
    w_out,
):
    q_width = w_query.shape[2]
    k_width = w_key.shape[2]
    left_width = q_width + 2 * k_width
    full_in, full_o = gather_weights(
        jnp.concatenate([w_query[0], w_key[0], w_value[0]], axis=1), w_out[0]
    )
    full_in = full_in.reshape(-1, left_width)
    full_o = full_o.reshape(-1, w_out.shape[2])
    weights = (full_in, full_o)
    norm_scale = norm_gain
    qk_gains = qk_gain[0]
    row_count = fwd_input.shape[1]
    cos_tab, sin_tab = rope_tables(row_count, HD)
    tables = jnp.stack(
        [
            jnp.concatenate([cos_tab, cos_tab], axis=1),
            jnp.concatenate([-sin_tab, sin_tab], axis=1),
        ]
    )
    tables = jnp.tile(tables, (1, 2 * q_width // HD, 1))
    section_position_index = lax.axis_index("section")
    section_total = lax.axis_size("section")
    bit_order = list(range(section_total.bit_length() - 1))
    reloaded = stash[0]
    for bit_index in bit_order:
        reloaded = swapped(reloaded, "section", bit_index)
    first_slot = run_slot(
        fwd_input[0], reloaded[0], cotangent[0], norm_scale, weights, qk_gains, tables
    )
    arrived = passed_along(first_slot[0], "section", 1)
    second_input = jnp.where(section_position_index == 0, fresh_input, arrived)
    returned = passed_along(first_slot[1], "section", -1)
    second_cot = jnp.where(section_position_index == section_total - 1, fresh_cotangent, returned)
    second_slot = run_slot(
        second_input, reloaded[1], second_cot, norm_scale, weights, qk_gains, tables
    )
    out_activations = jnp.stack([first_slot[0], second_slot[0]])[None]
    grad_input = jnp.stack([first_slot[1], second_slot[1]])[None]
    grad_scale = 1.0 / math.sqrt(2 * row_count * lax.axis_size("dp"))
    contract = (((0,), (0,)), ((), ()))
    norm_term = first_slot[4] + second_slot[4]
    qk_term = first_slot[5] + second_slot[5]
    feature_rows = norm_term.shape[1] // HD
    small = jnp.concatenate(
        [norm_term.reshape(feature_rows, HD), qk_term, jnp.zeros((6, HD), jnp.float32)], axis=0
    )
    gathered, sliced, smalls = exchange_grads(
        first_slot[2], second_slot[2], first_slot[3], second_slot[3], small * grad_scale
    )
    gathered = gathered.reshape(-1, gathered.shape[-1])
    sliced = jnp.moveaxis(sliced, 2, 0).reshape(2, -1, sliced.shape[-1])
    norm_total = jnp.sum(smalls[0, :, :feature_rows], axis=0).reshape(-1)
    qk_total = jnp.sum(smalls[:, :, feature_rows : feature_rows + 2], axis=(0, 1))
    left_term = lax.dot_general(
        sliced[0], gathered[:, :left_width], contract, preferred_element_type=jnp.float32
    )
    right_term = lax.dot_general(
        sliced[1], gathered[:, left_width:], contract, preferred_element_type=jnp.float32
    )
    left_term = left_term * grad_scale
    right_term = right_term * grad_scale
    grad_query = left_term[:, :q_width][None]
    grad_key = left_term[:, q_width : q_width + k_width][None]
    grad_value = left_term[:, q_width + k_width :][None]
    grad_out = right_term[None]
    return (
        out_activations,
        grad_input,
        grad_query,
        grad_key,
        grad_value,
        grad_out,
        norm_total[None],
        qk_total[None],
    )


def solution(mesh):
    return jax.shard_map(
        local,
        mesh=mesh,
        in_specs=(
            P("section", "dp", None),
            P("dp", None),
            P("section", "dp", None),
            P("dp", None),
            P("section", None, "dp", None),
            P("section", None),
            P("section", None, None),
            P("section", "dp", "tensor"),
            P("section", "dp", "tensor"),
            P("section", "dp", "tensor"),
            P("section", "dp", "tensor"),
        ),
        out_specs=(
            P("section", None, "dp", None),
            P("section", None, "dp", None),
            P("section", "dp", "tensor"),
            P("section", "dp", "tensor"),
            P("section", "dp", "tensor"),
            P("section", "dp", "tensor"),
            P("section", None),
            P("section", None, None),
        ),
        check_vma=False,
    )
```

```python
import functools
import math

import jax
import jax.numpy as jnp
from jax import lax
from jax.experimental import pallas as pl
from jax.experimental.pallas import tpu as pltpu
from jax.sharding import PartitionSpec as P

HD = 128


EPSILON = 1e-06
THETA = 1000000.0


def swapped(block, axis, apart):
    count = lax.axis_size(axis)
    route = []
    for low in range(count):
        high = low | 1 << apart
        if high != low and high < count:
            route += [(low, high), (high, low)]
    return lax.ppermute(block, axis, route)


def passed_along(array, axis, by):
    count = lax.axis_size(axis)
    pairs = [(i, i + by) for i in range(count) if 0 <= i + by < count]
    return lax.ppermute(array, axis, pairs)


def grid_of(count):
    tall = 4 if count % 4 == 0 else 1
    return tall, count // tall


def meet(peers):
    barrier = pltpu.get_barrier_semaphore()
    for peer in peers:
        pl.semaphore_signal(barrier, inc=1, device_id=peer)
    pl.semaphore_wait(barrier, len(peers))


class Sends:
    def __init__(self, sems):
        self.sems = sems
        self.started = []

    def start(self, src, dst, recv, peer, cond=None):
        copy = pltpu.make_async_remote_copy(
            src_ref=src,
            dst_ref=dst,
            send_sem=self.sems.at[len(self.started)],
            recv_sem=recv,
            device_id=peer,
        )
        if cond is None:
            copy.start()
        else:
            pl.when(cond)(copy.start)
        self.started.append((cond, copy))

    def arrived(self, dst, recv, peer):
        pltpu.make_async_remote_copy(
            src_ref=dst, dst_ref=dst, send_sem=self.sems.at[0], recv_sem=recv, device_id=peer
        ).wait_recv()

    def finish(self):
        for cond, copy in self.started:
            if cond is None:
                copy.wait_send()
            else:
                pl.when(cond)(copy.wait_send)


def relayed(count, pieces, early):
    tall, wide = grid_of(count)
    plain = wide + 1 + (tall - 1) * 2 * wide
    first = wide + 1 + 2 * (wide - 1) + (tall - 1) * 2 * wide
    return (pieces - early) * plain + early * first


def neighbours(count):
    tall, wide = grid_of(count)
    me = lax.axis_index("dp")
    row, col = me // wide, me % wide
    across = [row * wide + (col + i) % wide for i in range(1, wide)]
    along = [((row + i) % tall) * wide + col for i in range(1, tall)]
    return me, row, across, along


def cut(src, full, depth, parts):
    part = depth // parts
    return [
        (src.at[pl.ds(i * part, part)], lambda j, i=i: full.at[j, pl.ds(i * part, part)])
        for i in range(parts)
    ]


class Relay:
    def __init__(self, count, pieces, early, sends, recv):
        self.tall, self.wide = grid_of(count)
        self.me, self.row, self.across, self.along = neighbours(count)
        self.pieces, self.early, self.sends, self.recv = pieces, early, sends, recv
        self.up, self.down = self.row < self.tall - 1, self.row > 0

    def pass_on(self, cond, c, shard, peer, own=False):
        src, dst = self.pieces[c]
        src = src if own else dst(shard)
        self.sends.start(src, dst(shard), self.recv.at[shard, c], {"dp": peer}, cond)

    def begin(self, chosen):
        for c in chosen:
            self.pass_on(self.up, c, self.me, self.me + self.wide, True)
            self.pass_on(self.down, c, self.me, self.me - self.wide, True)
            for peer in self.across:
                self.pass_on(None, c, self.me, peer, True)

    def take(self, cond, c, shard):
        arrive = functools.partial(
            self.sends.arrived, self.pieces[c][1](shard), self.recv.at[shard, c], {"dp": self.me}
        )
        if cond is None:
            arrive()
        else:
            pl.when(cond)(arrive)

    def hop(self, c, d):
        wide, me = self.wide, self.me
        shifts = [0] + [p - me for p in self.across] if c in self.early else [0]
        if d == 1:
            for shift in shifts[1:]:
                self.take(None, c, me + shift)
                self.pass_on(self.up, c, me + shift, me + wide)
                self.pass_on(self.down, c, me + shift, me - wide)
        for shift in shifts:
            for near, here, on, after in (
                (me - d * wide, self.row >= d, self.up, me + wide),
                (me + d * wide, self.row + d < self.tall, self.down, me - wide),
            ):
                self.take(here, c, near + shift)
                self.pass_on(here & on, c, near + shift, after)
                if c not in self.early:
                    for peer in self.across:
                        self.pass_on(here, c, near, peer)

    def run(self, chosen):
        for wave in range(len(chosen) + self.tall - 2):
            for d in range(1, self.tall):
                if 0 <= wave - d + 1 < len(chosen):
                    self.hop(chosen[wave - d + 1], d)

    def end(self, chosen):
        for c in chosen:
            if c in self.early:
                continue
            for other in self.across:
                for i in range(self.tall):
                    self.take(None, c, ((self.row + i) % self.tall) * self.wide + other % self.wide)


def weights_kernel(count, in_ref, out_ref, full_in, full_out, send, recv, own):
    me, row, across, along = neighbours(count)
    depth = in_ref.shape[0]
    meet([{"dp": j} for j in along + across])
    sends = Sends(send)
    pieces = cut(in_ref, full_in, depth, 4) + cut(out_ref, full_out, depth, 4)
    relay = Relay(count, pieces, (), sends, recv)
    order = list(range(8))
    relay.begin(order)
    mine = [
        pltpu.make_async_copy(in_ref, full_in.at[me], own.at[0]),
        pltpu.make_async_copy(out_ref, full_out.at[me], own.at[1]),
    ]
    for copy in mine:
        copy.start()
    relay.run(order)
    relay.end(order)
    for copy in mine:
        copy.wait()
    sends.finish()


def grads_kernel(
    count, cols_a, cols_b, acts_a, acts_b, small_ref, full, sliced, smalls, send, recv, own
):
    me, row, across, along = neighbours(count)
    core = lax.axis_index("tensor")
    depth = sliced.shape[-1]
    everyone = [{"dp": (me + i) % count} for i in range(1, count)]
    crossed = [{"dp": (me + i) % count, "tensor": 1 - core} for i in range(count)]
    meet(everyone + crossed)
    half = cols_a.shape[0] // 2
    pieces = [
        (cols.at[pl.ds(p * half, half)], lambda j, i=i, p=p: full.at[j, i, pl.ds(p * half, half)])
        for i, cols in enumerate((cols_a, cols_b))
        for p in range(2)
    ]
    acts = (acts_a, acts_b)
    sends = Sends(send)
    relay = Relay(count, pieces, (), sends, recv)
    relay.begin(range(4))
    for peer in everyone:
        block = pl.ds(pl.multiple_of(peer["dp"] * depth, depth), depth)
        for i in range(2):
            sends.start(acts[i].at[:, :, block], sliced.at[me, i], recv.at[me, 6 + i], peer)
    for peer in everyone + crossed:
        sends.start(small_ref, smalls.at[core, me], recv.at[me, 4 + core], peer)
    block = pl.ds(pl.multiple_of(me * depth, depth), depth)
    mine = [
        pltpu.make_async_copy(cols_a, full.at[me, 0], own.at[0]),
        pltpu.make_async_copy(cols_b, full.at[me, 1], own.at[1]),
        pltpu.make_async_copy(acts_a.at[:, :, block], sliced.at[me, 0], own.at[3]),
        pltpu.make_async_copy(acts_b.at[:, :, block], sliced.at[me, 1], own.at[4]),
        pltpu.make_async_copy(small_ref, smalls.at[core, me], own.at[2]),
    ]
    for copy in mine:
        copy.start()
    relay.run(range(4))
    relay.end(range(4))
    for peer in everyone:
        j = peer["dp"]
        for i in range(2):
            sends.arrived(sliced.at[j, i], recv.at[j, 6 + i], peer)
        sends.arrived(smalls.at[core, j], recv.at[j, 4 + core], peer)
    for peer in crossed:
        j = peer["dp"]
        sends.arrived(smalls.at[1 - core, j], recv.at[j, 5 - core], peer)
    for copy in mine:
        copy.wait()
    sends.finish()


ANY = pl.BlockSpec(memory_space=pl.ANY)


def gather_weights(w_in, w_out):
    count = lax.axis_size("dp")
    sent = relayed(count, 8, 0)
    return pl.pallas_call(
        functools.partial(weights_kernel, count),
        out_shape=[jax.ShapeDtypeStruct((count,) + w.shape, w.dtype) for w in (w_in, w_out)],
        in_specs=[ANY] * 2,
        out_specs=[ANY] * 2,
        scratch_shapes=[
            pltpu.SemaphoreType.DMA((sent,)),
            pltpu.SemaphoreType.DMA((count, 8)),
            pltpu.SemaphoreType.DMA((2,)),
        ],
        compiler_params=pltpu.CompilerParams(collective_id=0, has_side_effects=True),
    )(w_in, w_out)


def exchange_grads(cols, cols_b, acts, acts_b, small):
    count = lax.axis_size("dp")
    rows, width = acts.shape[1:]
    sent = relayed(count, 4, 0) + 4 * count - 3
    return pl.pallas_call(
        functools.partial(grads_kernel, count),
        out_shape=[
            jax.ShapeDtypeStruct((count, 2) + cols.shape, cols.dtype),
            jax.ShapeDtypeStruct((count, 2, 2, rows, width // count), acts.dtype),
            jax.ShapeDtypeStruct((2, count) + small.shape, small.dtype),
        ],
        in_specs=[ANY] * 5,
        out_specs=[ANY] * 3,
        scratch_shapes=[
            pltpu.SemaphoreType.DMA((sent,)),
            pltpu.SemaphoreType.DMA((count, 8)),
            pltpu.SemaphoreType.DMA((5,)),
        ],
        compiler_params=pltpu.CompilerParams(collective_id=1, has_side_effects=True),
    )(cols, cols_b, acts, acts_b, small)


def rope_tables(length, width):
    half_width = width // 2
    freqs = jnp.exp(jnp.arange(half_width, dtype=jnp.float32) * (-2.0 * math.log(THETA) / width))
    angles = jnp.arange(length, dtype=jnp.float32)[:, None] * freqs[None, :]
    return (jnp.cos(angles), jnp.sin(angles))


def nt(left, right):
    return lax.dot_general(
        left, right, (((1,), (1,)), ((), ())), preferred_element_type=jnp.float32
    )


def tn(left, right):
    return lax.dot_general(
        left, right, (((0,), (0,)), ((), ())), preferred_element_type=jnp.float32
    )


def nn(left, right):
    return jnp.dot(left, right, preferred_element_type=jnp.float32)


def turn(vectors, tables, sign):
    cos_tab = tables[0, : vectors.shape[0]]
    sin_tab = tables[1, : vectors.shape[0]]
    return vectors * cos_tab + pltpu.roll(vectors, HD // 2, 1) * (sign * sin_tab)


def head_norm(raw_heads):
    inverse = lax.rsqrt(jnp.mean(raw_heads * raw_heads, axis=-1, keepdims=True) + EPSILON)
    return (raw_heads * inverse, inverse)


def unit_back(grad_unit, unit_row_vectors, inverse):
    return inverse * (
        grad_unit
        - unit_row_vectors * jnp.mean(grad_unit * unit_row_vectors, axis=-1, keepdims=True)
    )


def tall_heads(wide):
    return jnp.concatenate(
        [wide[:, h * HD : (h + 1) * HD] for h in range(wide.shape[1] // HD)], axis=0
    )


def wide_heads(tall, rows):
    return jnp.concatenate(
        [tall[h * rows : (h + 1) * rows] for h in range(tall.shape[0] // rows)], axis=1
    )


def lower(tall, rows):
    return jnp.concatenate(
        [tall[h + rows : h + 2 * rows] for h in range(0, tall.shape[0], 2 * rows)], axis=0
    )


def slot_kernel(
    xf_ref, xb_ref, g_ref, gain_ref, qk_ref, tables, wi_ref, wo_ref,
    parts_ref, cols_ref, acts_ref, terms_ref,
):
    rows = xf_ref.shape[0]
    q_width = wo_ref.shape[1]
    scale = 1.0 / math.sqrt(HD)
    q_gain, k_gain = qk_ref[0:1], qk_ref[1:2]
    x = jnp.concatenate([xf_ref[...], xb_ref[...]], axis=0).astype(jnp.float32)
    unit, _ = head_norm(x)
    normed = (unit * gain_ref[...]).astype(jnp.bfloat16)
    acts_ref[0] = normed[rows:]
    acts_ref[1] = g_ref[...]
    qkv = nn(normed, wi_ref[...])
    q_unit, q_inv = head_norm(tall_heads(qkv[:, :q_width]))
    k_unit, k_inv = head_norm(qkv[:, q_width : q_width + HD])
    values = qkv[:, q_width + HD :].astype(jnp.bfloat16)
    queries = turn(q_unit * q_gain, tables, 1.0).astype(jnp.bfloat16)
    keys = turn(k_unit * k_gain, tables, 1.0).astype(jnp.bfloat16)
    scores = nt(queries, keys) * scale
    row = lax.rem(lax.broadcasted_iota(jnp.int32, scores.shape, 0), 2 * rows)
    col = lax.broadcasted_iota(jnp.int32, scores.shape, 1)
    seen = (row >= col) & ((row < rows) | (col >= rows))
    expd = jnp.where(seen, jnp.exp(scores), 0.0)
    probs = expd / jnp.sum(expd, axis=-1, keepdims=True)
    probs_b = probs.astype(jnp.bfloat16)
    attended = wide_heads(nn(probs_b, values), 2 * rows).astype(jnp.bfloat16)
    parts_ref[:rows] = nt(attended[:rows], wo_ref[...]).astype(jnp.bfloat16)
    d_attn = tall_heads(nn(g_ref[...], wo_ref[...])).astype(jnp.bfloat16)
    probs, q_unit, q_inv = lower(probs, rows), lower(q_unit, rows), lower(q_inv, rows)
    probs_b, queries = lower(probs_b, rows), lower(queries, rows)
    d_probs = nt(d_attn, values)
    d_scores = probs * (d_probs - jnp.sum(probs * d_probs, axis=-1, keepdims=True)) * scale
    d_scores = d_scores.astype(jnp.bfloat16)
    d_value = tn(probs_b, d_attn)[rows:].astype(jnp.bfloat16)
    d_query = turn(nn(d_scores, keys), tables, -1.0)
    d_key = turn(tn(d_scores, queries)[rows:], tables, -1.0)
    k_unit, k_inv = k_unit[rows:], k_inv[rows:]
    terms_ref[0:1] = jnp.sum(d_query * q_unit, axis=0, keepdims=True)
    terms_ref[1:2] = jnp.sum(d_key * k_unit, axis=0, keepdims=True)
    q_grad = wide_heads(unit_back(d_query * q_gain, q_unit, q_inv), rows).astype(jnp.bfloat16)
    k_grad = unit_back(d_key * k_gain, k_unit, k_inv).astype(jnp.bfloat16)
    columns = jnp.concatenate([q_grad, k_grad, d_value], axis=1)
    cols_ref[:, : columns.shape[1]] = columns
    cols_ref[:, columns.shape[1] :] = attended[rows:]
    parts_ref[rows:] = nt(columns, wi_ref[...]).astype(jnp.bfloat16)


def finish_kernel(xf_ref, xb_ref, g_ref, gain_ref, mine_ref, other_ref, out_ref, back_ref, term_ref):
    rows = xf_ref.shape[0]
    total = mine_ref[...].astype(jnp.float32) + other_ref[...].astype(jnp.float32)
    out_ref[...] = (xf_ref[...].astype(jnp.float32) + total[:rows]).astype(jnp.bfloat16)
    unit, inverse = head_norm(xb_ref[...].astype(jnp.float32))
    d_normed = total[rows:]
    d_input = g_ref[...].astype(jnp.float32) + unit_back(d_normed * gain_ref[...], unit, inverse)
    back_ref[...] = d_input.astype(jnp.bfloat16)
    term_ref[...] = jnp.sum(d_normed * unit, axis=0, keepdims=True)


ROOM = pltpu.CompilerParams(vmem_limit_bytes=48 * 1024 * 1024)


def run_slot(x_forward, x_backward, cot_rows, norm_scale, weights, qk_gains, tables):
    rows, width = x_forward.shape
    w_in, w_out = weights
    shape = jax.ShapeDtypeStruct
    parts, cols, acts, terms = pl.pallas_call(
        slot_kernel,
        out_shape=[
            shape((2 * rows, width), jnp.bfloat16),
            shape((rows, w_in.shape[1] + w_out.shape[1]), jnp.bfloat16),
            shape((2, rows, width), jnp.bfloat16),
            shape((2, HD), jnp.float32),
        ],
        compiler_params=ROOM,
    )(x_forward, x_backward, cot_rows, norm_scale, qk_gains, tables, w_in, w_out)
    other = lax.ppermute(parts, "tensor", [(0, 1), (1, 0)])
    layer_out, d_input, norm_term = pl.pallas_call(
        finish_kernel,
        out_shape=[
            shape((rows, width), jnp.bfloat16),
            shape((rows, width), jnp.bfloat16),
            shape((1, width), jnp.float32),
        ],
        compiler_params=ROOM,
    )(x_forward, x_backward, cot_rows, norm_scale, parts, other)
    return layer_out, d_input, cols, acts, norm_term, terms


def local(
    fwd_input,
    fresh_input,
    cotangent,
    fresh_cotangent,
    stash,
    norm_gain,
    qk_gain,
    w_query,
    w_key,
    w_value,
    w_out,
):
    q_width = w_query.shape[2]
    k_width = w_key.shape[2]
    left_width = q_width + 2 * k_width
    full_in, full_o = gather_weights(
        jnp.concatenate([w_query[0], w_key[0], w_value[0]], axis=1), w_out[0]
    )
    full_in = full_in.reshape(-1, left_width)
    full_o = full_o.reshape(-1, w_out.shape[2])
    weights = (full_in, full_o)
    norm_scale = norm_gain
    qk_gains = qk_gain[0]
    row_count = fwd_input.shape[1]
    cos_tab, sin_tab = rope_tables(row_count, HD)
    tables = jnp.stack(
        [
            jnp.concatenate([cos_tab, cos_tab], axis=1),
            jnp.concatenate([-sin_tab, sin_tab], axis=1),
        ]
    )
    tables = jnp.tile(tables, (1, 2 * q_width // HD, 1))
    section_position_index = lax.axis_index("section")
    section_total = lax.axis_size("section")
    bit_order = list(range(section_total.bit_length() - 1))
    reloaded = stash[0]
    for bit_index in bit_order:
        reloaded = swapped(reloaded, "section", bit_index)
    first_slot = run_slot(
        fwd_input[0], reloaded[0], cotangent[0], norm_scale, weights, qk_gains, tables
    )
    arrived = passed_along(first_slot[0], "section", 1)
    second_input = jnp.where(section_position_index == 0, fresh_input, arrived)
    returned = passed_along(first_slot[1], "section", -1)
    second_cot = jnp.where(section_position_index == section_total - 1, fresh_cotangent, returned)
    second_slot = run_slot(
        second_input, reloaded[1], second_cot, norm_scale, weights, qk_gains, tables
    )
    out_activations = jnp.stack([first_slot[0], second_slot[0]])[None]
    grad_input = jnp.stack([first_slot[1], second_slot[1]])[None]
    grad_scale = 1.0 / math.sqrt(2 * row_count * lax.axis_size("dp"))
    contract = (((0,), (0,)), ((), ()))
    norm_term = first_slot[4] + second_slot[4]
    qk_term = first_slot[5] + second_slot[5]
    feature_rows = norm_term.shape[1] // HD
    small = jnp.concatenate(
        [norm_term.reshape(feature_rows, HD), qk_term, jnp.zeros((6, HD), jnp.float32)], axis=0
    )
    gathered, sliced, smalls = exchange_grads(
        first_slot[2], second_slot[2], first_slot[3], second_slot[3], small * grad_scale
    )
    gathered = gathered.reshape(-1, gathered.shape[-1])
    sliced = jnp.moveaxis(sliced, 2, 0).reshape(2, -1, sliced.shape[-1])
    norm_total = jnp.sum(smalls[0, :, :feature_rows], axis=0).reshape(-1)
    qk_total = jnp.sum(smalls[:, :, feature_rows : feature_rows + 2], axis=(0, 1))
    left_term = lax.dot_general(
        sliced[0], gathered[:, :left_width], contract, preferred_element_type=jnp.float32
    )
    right_term = lax.dot_general(
        sliced[1], gathered[:, left_width:], contract, preferred_element_type=jnp.float32
    )
    left_term = left_term * grad_scale
    right_term = right_term * grad_scale
    grad_query = left_term[:, :q_width][None]
    grad_key = left_term[:, q_width : q_width + k_width][None]
    grad_value = left_term[:, q_width + k_width :][None]
    grad_out = right_term[None]
    return (
        out_activations,
        grad_input,
        grad_query,
        grad_key,
        grad_value,
        grad_out,
        norm_total[None],
        qk_total[None],
    )


def solution(mesh):
    return jax.shard_map(
        local,
        mesh=mesh,
        in_specs=(
            P("section", "dp", None),
            P("dp", None),
            P("section", "dp", None),
            P("dp", None),
            P("section", None, "dp", None),
            P("section", None),
            P("section", None, None),
            P("section", "dp", "tensor"),
            P("section", "dp", "tensor"),
            P("section", "dp", "tensor"),
            P("section", "dp", "tensor"),
        ),
        out_specs=(
            P("section", None, "dp", None),
            P("section", None, "dp", None),
            P("section", "dp", "tensor"),
            P("section", "dp", "tensor"),
            P("section", "dp", "tensor"),
            P("section", "dp", "tensor"),
            P("section", None),
            P("section", None, None),
        ),
        check_vma=False,
    )
```
